256 devices in a mesh: gx: 16 (over z, core), gy: 4 (over y), gz: 4 (over x).
Axes of the slice: x: 4, y: 4, z: 8, core: 2. Of those that a mesh axis runs over, the one named last changes fastest.
Arguments:
- start_state: float32 [16, 64, 32, 512], P(None, 'gx', 'gz', 'gy'), may hold values from -6 to 6
- cotangent: float32 [16, 64, 32, 512], P(None, 'gx', 'gz', 'gy'), may hold values from -6 to 6
- update_masks: int32 [2, 64, 32, 512], P(None, 'gx', 'gz', 'gy'), may hold values 0 or 1
- first_weight: float32 [48, 64], replicated, may hold values from -0.875 to 0.875
- first_bias: float32 [64], replicated, may hold values from -3 to 3
- second_weight: float32 [64, 16], replicated, may hold values from -0.75 to 0.75
- second_bias: float32 [16], replicated, may hold values from -3 to 3
Outputs:
- grad_state: float32 [16, 64, 32, 512], P(None, 'gx', 'gz', 'gy')
- grad_first_weight: float32 [48, 64], replicated
- grad_first_bias: float32 [64], replicated
- grad_second_weight: float32 [64, 16], replicated
- grad_second_bias: float32 [16], replicated
The draws below stay inside these ranges and needn't reach their ends.
Inputs may be any that keep to these rules, and one draw needn't show every extreme that they name: `update_masks`: a flag for each cell and step.
All inputs are finite; a program needn't handle non-finite values. No bound on the sum of `update_masks` on one device may be relied on, other than what follows from the above.
Results may differ from the reference program's by a relative error of at most 0.0003.
Values sent between devices are 32-bit elements; how exact they have to be, the bound alone decides.
A program may use at most 64 MiB of HBM per device.

```python
import math
import jax
import jax.numpy as jnp
from jax import lax

CH = 16
HID = 64
PERC = 48
STEPS = 2
CX = 4
NX = 64
NY = 512
NZ = 32


def place_ends(array, own_key, least, top_value):
    longest = array.shape.index(max(array.shape))
    spots = []
    for shift in (0, 1):
        where = [jax.random.randint(jax.random.fold_in(own_key, axis), (), 0, length) for axis, length in enumerate(array.shape)]
        where[longest] = (where[longest] + shift) % array.shape[longest]
        spots.append(tuple(where))
    return array.at[spots[0]].set(least).at[spots[1]].set(top_value)


def block_levels(key, dims, split, low, largest):
    gain, own = 1.0, jax.random.fold_in(key, 6)
    for dim, shards_of in split:
        steps = jnp.exp(jax.random.uniform(jax.random.fold_in(own, dim), (shards_of,), jnp.float32, low / len(split), largest / len(split)))
        gain = gain * jnp.repeat(steps, dims[dim] // shards_of).reshape([-1 if axis == dim else 1 for axis in range(len(dims))])
    return gain


def noise(rng, extent, scale, most, cuts=(), kind=jnp.bfloat16):
    loudness = block_levels(rng, extent, cuts, -0.22, 0.18) if cuts else 1.0
    array = jax.random.normal(rng, extent, jnp.float32) * scale * loudness
    return jnp.minimum(jnp.maximum(array, -most), most).astype(kind)


def setup_inputs(seed: int = 0) -> dict:
    streams_of = jax.random.split(jax.random.key(seed), 8)
    return {
        "start_state": noise(streams_of[0], (CH, NX, NZ, NY), 1.0, 6.0, ((1, 16), (2, 4), (3, 4)), jnp.float32),
        "cotangent": noise(streams_of[1], (CH, NX, NZ, NY), 1.0, 6.0, ((1, 16), (2, 4), (3, 4)), jnp.float32),
        "update_masks": place_ends((jax.random.randint(streams_of[2], (STEPS, NX, NZ, NY), 0, 2) < 1).astype(jnp.int32), jax.random.fold_in(streams_of[2], 1), 0, 1),
        "first_weight": noise(streams_of[3], (PERC, HID), PERC ** -0.5, 0.875, (), jnp.float32),
        "first_bias": noise(streams_of[4], (HID,), 0.5, 3.0, (), jnp.float32),
        "second_weight": noise(streams_of[5], (HID, CH), HID ** -0.5, 0.75, (), jnp.float32),
        "second_bias": noise(streams_of[6], (CH,), 0.5, 3.0, (), jnp.float32),
    }


highest = lax.Precision.HIGHEST

def shifted(field, axis, start):
    return lax.slice_in_dim(field, start, field.shape[axis] - 2 + start, axis=axis)

def differ(field, axis):
    return shifted(field, axis, 2) - shifted(field, axis, 0)

def smooth(field, axis):
    return shifted(field, axis, 0) + 2.0 * shifted(field, axis, 1) + shifted(field, axis, 2)

def along_x(field):
    return smooth(smooth(differ(field, 1), 2), 3) * 0.125

def along_y(field):
    return smooth(smooth(differ(field, 3), 1), 2) * 0.125

def along_z(field):
    return smooth(smooth(differ(field, 2), 1), 3) * 0.125

def sobel(field):
    return jnp.concatenate([along_x(field), along_y(field), along_z(field)], axis=0)

def sobel_adjoint(grads, chans):
    return -(along_x(grads[:chans]) + along_y(grads[chans:2 * chans]) + along_z(grads[2 * chans:]))

def hidden_of(perc, first_weight, first_bias):
    return jnp.tanh(jnp.einsum('kh,kxzy->hxzy', first_weight, perc, precision=highest) + first_bias[:, None, None, None])

def update_of(hidden, second_weight, second_bias):
    return jnp.einsum('ho,hxzy->oxzy', second_weight, hidden, precision=highest) + second_bias[:, None, None, None]

def crop(field, margin):
    if margin == 0:
        return field
    return field[:, margin:-margin, margin:-margin, margin:-margin]

def backward_cells(perc, hidden, masked, first_weight, second_weight, margin):
    hid_grad = jnp.einsum('ho,oxzy->hxzy', second_weight, masked, precision=highest)
    pre_grad = hid_grad * (1.0 - hidden * hidden)
    perc_grad = jnp.einsum('kh,hxzy->kxzy', first_weight, pre_grad, precision=highest)
    inner_pre = crop(pre_grad, margin)
    inner_masked = crop(masked, margin)
    grads = (jnp.einsum('kxzy,hxzy->kh', crop(perc, margin), inner_pre, precision=highest), lax.optimization_barrier(jnp.sum(inner_pre, axis=(1, 2, 3))), jnp.einsum('hxzy,oxzy->ho', crop(hidden, margin), inner_masked, precision=highest), lax.optimization_barrier(jnp.sum(inner_masked, axis=(1, 2, 3))))
    return (perc_grad, grads)

def reference(start_state, cotangent, update_masks, first_weight, first_bias, second_weight, second_bias):
    chans = start_state.shape[0]
    block = CX
    count = NX // block
    masks_float = update_masks.astype(jnp.float32)
    indices = jnp.arange(count, dtype=jnp.int32)

    def forward_step(state, mask):
        padded = jnp.pad(state, ((0, 0), (1, 1), (1, 1), (1, 1)))

        def one_block(index):
            start = (index * block).astype(jnp.int32)
            slab = lax.dynamic_slice_in_dim(padded, start, block + 2, axis=1)
            hidden = hidden_of(sobel(slab), first_weight, first_bias)
            update = update_of(hidden, second_weight, second_bias)
            own = lax.dynamic_slice_in_dim(state, start, block, axis=1)
            own_mask = lax.dynamic_slice_in_dim(mask, start, block, axis=0)
            return own + own_mask[None] * update
        blocks = lax.map(one_block, indices)
        return jnp.moveaxis(blocks, 0, 1).reshape(state.shape)

    def backward_step(state, mask, carried):
        padded = jnp.pad(state, ((0, 0), (2, 2), (2, 2), (2, 2)))
        mask_pad = jnp.pad(mask, ((2, 2), (2, 2), (2, 2)))
        carried_pad = jnp.pad(carried, ((0, 0), (2, 2), (2, 2), (2, 2)))

        def one_block(index):
            start = (index * block).astype(jnp.int32)
            slab = lax.dynamic_slice_in_dim(padded, start, block + 4, axis=1)
            perc = sobel(slab)
            hidden = hidden_of(perc, first_weight, first_bias)
            mask_slab = lax.dynamic_slice_in_dim(mask_pad, start + 1, block + 2, axis=0)[:, 1:-1, 1:-1]
            carried_slab = lax.dynamic_slice_in_dim(carried_pad, start + 1, block + 2, axis=1)[:, :, 1:-1, 1:-1]
            masked = mask_slab[None] * carried_slab
            perc_grad, grads = backward_cells(perc, hidden, masked, first_weight, second_weight, 1)
            own = lax.dynamic_slice_in_dim(carried, start, block, axis=1) + sobel_adjoint(perc_grad, chans)
            return (own, grads)
        blocks, grads = lax.map(one_block, indices)
        result = jnp.moveaxis(blocks, 0, 1).reshape(carried.shape)
        return (result, tuple((lax.optimization_barrier(jnp.sum(piece, axis=0)) for piece in grads)))
    states = [start_state]
    for step in range(update_masks.shape[0] - 1):
        states.append(forward_step(states[-1], masks_float[step]))
    carried = cotangent
    totals = None
    for step in range(update_masks.shape[0] - 1, -1, -1):
        carried, grads = backward_step(states[step], masks_float[step], carried)
        totals = grads if totals is None else tuple((a + b for a, b in zip(totals, grads)))
    scale = 1.0 / math.sqrt(NX * NY * NZ)
    return (carried, totals[0] * scale, totals[1] * scale, totals[2] * scale, totals[3] * scale)
```

```python
import functools
import math

import jax
import jax.numpy as jnp
from jax import lax
from jax.experimental import pallas as pl
from jax.experimental.pallas import tpu as pltpu
from jax.sharding import PartitionSpec as P

MESH = pl.DeviceIdType.MESH
F32 = jnp.float32
BF16 = jnp.bfloat16

CH, HID, PERC = 16, 64, 48
BX, BZ, BY = 4, 8, 128
ROW = BZ * BY

P_ROWS = 2 * PERC + 16 + PERC
H_ROWS = 2 * HID + 16 + HID

DIRS = [(dx, dy, dz) for dx in (-1, 0, 1) for dy in (-1, 0, 1) for dz in (-1, 0, 1) if (dx, dy, dz) != (0, 0, 0)]
FLAT = [d for d in DIRS if d[1] == 0]
TALL = [d for d in DIRS if d[1] != 0]


def high(value):
    return value.astype(BF16).astype(F32)


def split3(value):
    first = high(value)
    second = high(value - first)
    return first, second, value - first - second


def span(step, length, kind):
    if step == 0:
        return pl.ds(1, length)
    if kind == "own":
        return pl.ds(1 if step < 0 else length, 1)
    return pl.ds(0 if step < 0 else length + 1, 1)


def dot(a, b):
    return lax.dot_general(a, b, (((1,), (0,)), ((), ())), preferred_element_type=F32)


def dot_nt(a, b):
    return lax.dot_general(a, b, (((1,), (1,)), ((), ())), preferred_element_type=F32)


def kernel(
    sizes,
    state_ref, cot_ref, mask_ref, w1_ref, b1_ref, w2_ref, b2_ref,
    grad_ref, gw1_ref, gb1_ref, gw2_ref, gb2_ref,
    field, packs, halos, outs, opacks, rx, rz, rc, rpacks,
    percs, hids, hidden, dzs, dus, carried, zf, placed, onehot,
    tall, l1, l2, l3, l4, turn, sums, src1, rx1, rx2, rx3,
    send_sem, recv_sem, ar_send, ar_recv,
):
    nx, ny, nz = sizes
    gx, gy, gz = lax.axis_index("gx"), lax.axis_index("gy"), lax.axis_index("gz")

    def device(offset):
        ox, oy, oz = offset
        return (
            lax.rem(gx + (ox % nx), nx) if ox % nx else gx,
            lax.rem(gy + (oy % ny), ny) if oy % ny else gy,
            lax.rem(gz + (oz % nz), nz) if oz % nz else gz,
        )

    plane = [(0, a, b) for a in range(ny) for b in range(nz) if (a, b) != (0, 0)]
    line = [(a, 0, 0) for a in range(1, nx)]
    partners = []
    for o in DIRS + plane + line:
        o = (o[0] % nx, o[1] % ny, o[2] % nz)
        if o not in partners:
            partners.append(o)

    barrier = pltpu.get_barrier_semaphore()
    for o in partners:
        pl.semaphore_signal(barrier, inc=1, device_id=device(o), device_id_type=MESH)

    lane = lax.broadcasted_iota(jnp.int32, (8, 128), 1)
    sub = lax.broadcasted_iota(jnp.int32, (8, 128), 0)
    lane3 = lax.broadcasted_iota(jnp.int32, (1, 1, 128), 2)
    not_first = (lane3 > 0).astype(F32)
    not_last = (lane3 < 127).astype(F32)

    def pack_state(k):
        def body(x, _):
            tile = field[k, x + 1, pl.ds(1, BZ)].reshape(128, 128)
            turned = tile.T
            packs[k, pl.ds(x, 1), :] = turned[0:1, :]
            packs[k, pl.ds(x + 4, 1), :] = turned[127:128, :]
            return 0
        lax.fori_loop(0, BX, body, 0)

    for x in range(BX):
        for z in range(BZ):
            field[0, x + 1, z + 1] = state_ref[pl.ds(x * BZ + z, CH, stride=BX * BZ), :]
    pack_state(0)

    def state_copies(k):
        copies = []
        for d in FLAT:
            i = DIRS.index(d)
            copies.append(pltpu.make_async_remote_copy(
                src_ref=field.at[k, span(d[0], BX, "own"), span(d[2], BZ, "own")],
                dst_ref=field.at[k, span(-d[0], BX, "halo"), span(-d[2], BZ, "halo")],
                send_sem=send_sem.at[k, i], recv_sem=recv_sem.at[k, i],
                device_id=device(d), device_id_type=MESH))
        for d in TALL:
            i = DIRS.index(d)
            copies.append(pltpu.make_async_remote_copy(
                src_ref=packs.at[k],
                dst_ref=halos.at[k, 0 if d[1] > 0 else 1, 1 - d[0], 1 - d[2]],
                send_sem=send_sem.at[k, i], recv_sem=recv_sem.at[k, i],
                device_id=device(d), device_id_type=MESH))
        return copies

    def out_copies(k):
        copies = []
        for d in FLAT:
            i = DIRS.index(d)
            if d[0] and d[2]:
                dst = rc.at[k, pl.ds(0 if d[0] > 0 else 1, 1), pl.ds(0 if d[2] > 0 else 1, 1)]
            elif d[0]:
                dst = rx.at[k, pl.ds(0 if d[0] > 0 else 1, 1)]
            else:
                dst = rz.at[k, :, pl.ds(0 if d[2] > 0 else 1, 1)]
            copies.append(pltpu.make_async_remote_copy(
                src_ref=outs.at[k, span(d[0], BX, "halo"), span(d[2], BZ, "halo")],
                dst_ref=dst,
                send_sem=send_sem.at[2 + k, i], recv_sem=recv_sem.at[2 + k, i],
                device_id=device(d), device_id_type=MESH))
        for d in TALL:
            i = DIRS.index(d)
            copies.append(pltpu.make_async_remote_copy(
                src_ref=opacks.at[k, 0 if d[1] < 0 else 1],
                dst_ref=rpacks.at[k, 0 if d[1] > 0 else 1, 1 - d[0], 1 - d[2]],
                send_sem=send_sem.at[2 + k, i], recv_sem=recv_sem.at[2 + k, i],
                device_id=device(d), device_id_type=MESH))
        return copies

    pl.semaphore_wait(barrier, len(partners))
    first = state_copies(0)
    for c in first:
        c.start()

    tall[...] = jnp.zeros_like(tall)
    w1 = w1_ref[...] * 0.125
    w1h = high(w1)
    tall[0:48, 0:64] = w1h
    tall[48:96, 0:64] = w1h
    b1 = split3(b1_ref[...])
    for s in range(3):
        tall[96 + s : 97 + s, 0:64] = b1[s]
    tall[112:160, 0:64] = w1 - w1h
    l1[...] = tall[...].T[0:64, 0:P_ROWS].astype(BF16)

    tall[...] = jnp.zeros_like(tall)
    w2 = w2_ref[...]
    w2h = high(w2)
    tall[0:64, 0:16] = w2h
    tall[64:128, 0:16] = w2h
    b2 = split3(b2_ref[...])
    for s in range(3):
        tall[128 + s : 129 + s, 0:16] = b2[s]
    tall[144:208, 0:16] = w2 - w2h
    l2[...] = tall[...].T[0:16, 0:H_ROWS].astype(BF16)

    tall[...] = jnp.zeros_like(tall)
    tall[0:48, 0:64] = -w1
    w1t = tall[...].T[0:64, 0:48]
    tall[...] = jnp.zeros_like(tall)
    w1th = high(w1t)
    tall[0:64, 0:48] = w1th
    tall[64:128, 0:48] = w1th
    tall[128:192, 0:48] = w1t - w1th
    l4[...] = tall[...].T[0:48, 0:192].astype(BF16)

    tall[...] = jnp.zeros_like(tall)
    tall[0:64, 0:16] = w2
    w2t = tall[...].T[0:16, 0:64]
    tall[...] = jnp.zeros_like(tall)
    w2th = high(w2t)
    tall[0:16, 0:64] = w2th
    tall[16:32, 0:64] = w2th
    tall[32:48, 0:64] = w2t - w2th
    l3[...] = tall[...].T[0:64, 0:48].astype(BF16)

    kk = lax.broadcasted_iota(jnp.int32, (128, 128), 0)
    yy = lax.broadcasted_iota(jnp.int32, (128, 128), 1)
    feature = lax.rem(lax.div(kk, 8), 3)
    row8 = lax.rem(kk, 8)
    hit = jnp.logical_and(kk < 72, yy == jnp.where(row8 < 4, 127, 0))
    for x in range(BX):
        for f in range(3):
            sign = jnp.where(row8 < 4, 1.0, -1.0) if f == 1 else 1.0
            onehot[x * 3 + f] = jnp.where(
                jnp.logical_and(hit, jnp.logical_and(feature == f, lax.rem(row8, 4) == x)), sign, 0.0
            ).astype(BF16)
    turn[...] = jnp.zeros_like(turn)
    for k in range(2):
        for x in range(BX):
            percs[k, x, 2 * PERC : 2 * PERC + 16, :] = jnp.ones((16, ROW), BF16)
            hids[k, x, 2 * HID : 2 * HID + 16, :] = jnp.ones((16, ROW), BF16)
    for x in (0, 1, BX + 2, BX + 3):
        zf[x] = jnp.zeros_like(zf[x])
    for x in range(BX):
        for z in range(BZ):
            carried[x, z] = cot_ref[pl.ds(x * BZ + z, CH, stride=BX * BZ), :]

    low_x, top_x = (gx > 0).astype(F32), (gx < nx - 1).astype(F32)
    low_y, top_y = (gy > 0).astype(F32), (gy < ny - 1).astype(F32)
    low_z, top_z = (gz > 0).astype(F32), (gz < nz - 1).astype(F32)
    in_x, in_z = (low_x, 1.0, top_x), (low_z, 1.0, top_z)

    def store_split(ref, lead, rows, value, again):
        hi = value.astype(BF16)
        lo = (value - hi.astype(F32)).astype(BF16)
        ref[(*lead, pl.ds(0, rows))] = hi
        ref[(*lead, pl.ds(rows, rows))] = lo
        ref[(*lead, pl.ds(again, rows))] = hi

    def place(rows24, features):
        parts = split3(rows24)
        n = 8 * features
        for s in range(3):
            turn[24 * s : 24 * s + n, :] = parts[s]
        turned = turn[...].T.astype(BF16)
        for x in range(BX):
            for f in range(features):
                placed[x * 3 + f] = dot(turned, onehot[x * 3 + f])

    def clear_outside(k):
        @pl.when(gx == 0)
        def _():
            field[k, 0] = jnp.zeros_like(field[k, 0])
        @pl.when(gx == nx - 1)
        def _():
            field[k, BX + 1] = jnp.zeros_like(field[k, BX + 1])
        @pl.when(gz == 0)
        def _():
            field[k, :, 0] = jnp.zeros_like(field[k, :, 0])
        @pl.when(gz == nz - 1)
        def _():
            field[k, :, BZ + 1] = jnp.zeros_like(field[k, :, BZ + 1])

    def filter_columns(k):
        grid = {}
        for ix in range(3):
            for iz in range(3):
                tile = jnp.where(sub < 4, halos[k, 1, ix, iz] * top_y, halos[k, 0, ix, iz] * low_y)
                grid[ix, iz] = tile * (in_x[ix] * in_z[iz])
        xs, xd = [], []
        for iz in range(3):
            mid = grid[1, iz]
            after = pltpu.roll(jnp.where(lax.rem(sub, 4) == 0, pltpu.roll(grid[2, iz], 4, 0), mid), 7, 0)
            before = pltpu.roll(jnp.where(lax.rem(sub, 4) == 3, pltpu.roll(grid[0, iz], 4, 0), mid), 1, 0)
            xs.append(before + 2.0 * mid + after)
            xd.append(after - before)

        def around(t):
            above = pltpu.roll(jnp.where(lane < 16, t[2], t[1]), 112, 1)
            below = pltpu.roll(jnp.where(lane >= 112, t[0], t[1]), 16, 1)
            return below, above

        d_below, d_above = around(xd)
        s_below, s_above = around(xs)
        place(jnp.concatenate([
            d_below + 2.0 * xd[1] + d_above,
            s_below + 2.0 * xs[1] + s_above,
            s_above - s_below], axis=0), 3)

    def forward(k):
        def body(x, _):
            zs, zd = [], []
            for i in range(3):
                v = field[k, x + i]
                zs.append(v[0:8] + 2.0 * v[1:9] + v[2:10])
                zd.append(v[2:10] - v[0:8])
            b = zs[2] - zs[0]
            a = zs[0] + 2.0 * zs[1] + zs[2]
            c = zd[0] + 2.0 * zd[1] + zd[2]
            up = lambda t: pltpu.roll(t, 127, 2) * not_last
            down = lambda t: pltpu.roll(t, 1, 2) * not_first
            features = (
                2.0 * b + up(b) + down(b),
                up(a) - down(a),
                2.0 * c + up(c) + down(c),
            )
            for f in range(3):
                perc = features[f] + placed[x * 3 + f].reshape(BZ, CH, BY)
                flat = jnp.concatenate([perc[z] for z in range(BZ)], axis=1)
                hi = flat.astype(BF16)
                lo = (flat - hi.astype(F32)).astype(BF16)
                percs[k, x, f * 16 : f * 16 + 16] = hi
                percs[k, x, 48 + f * 16 : 64 + f * 16] = lo
                percs[k, x, 112 + f * 16 : 128 + f * 16] = hi
            hid = jnp.tanh(dot(l1[...], percs[k, x]))
            hidden[k, x] = hid
            store_split(hids, (k, x), HID, hid, 2 * HID + 16)
            if k == 0:
                update = dot(l2[...], hids[k, x])
                mask = mask_ref[pl.ds(pl.multiple_of(x * BZ, 8), BZ), :].astype(F32)
                for z in range(BZ):
                    field[1, x + 1, z + 1] = field[0, x + 1, z + 1] + mask[z : z + 1] * update[:, z * BY : (z + 1) * BY]
            return 0
        lax.fori_loop(0, BX, body, 0)

    def cells(k):
        def body(x, _):
            mask = mask_ref[pl.ds(pl.multiple_of((k * BX + x) * BZ, 8), BZ), :].astype(F32)
            g = carried[x]
            du = jnp.concatenate([mask[z : z + 1] * g[z] for z in range(BZ)], axis=1)
            store_split(dus, (x,), CH, du, 2 * CH)
            hid = hidden[k, x]
            dz = dot(l3[...], dus[x]) * (1.0 - hid * hid)
            store_split(dzs, (x,), HID, dz, 2 * HID)
            return 0
        lax.fori_loop(0, BX, body, 0)

    def adjoint(k):
        def body(x, _):
            dp = dot(l4[...], dzs[x])
            zero = jnp.zeros((2, CH, BY), F32)
            for f in range(3):
                q = jnp.concatenate(
                    [zero] + [dp[f * 16 : f * 16 + 16, z * BY : (z + 1) * BY].reshape(1, CH, BY) for z in range(BZ)] + [zero], axis=0)
                zf[x + 2, f] = q[2:12] - q[0:10] if f == 2 else q[0:10] + 2.0 * q[1:11] + q[2:12]
            return 0
        lax.fori_loop(0, BX, body, 0)

        def plane_body(xo, _):
            pr = zf[xo + 2, 0] - zf[xo, 0] + zf[xo, 2] + 2.0 * zf[xo + 1, 2] + zf[xo + 2, 2]
            q = zf[xo, 1] + 2.0 * zf[xo + 1, 1] + zf[xo + 2, 1]
            up, down = pr + q, pr - q
            outs[k, xo] = 2.0 * pr + pltpu.roll(down, 1, 2) * not_first + pltpu.roll(up, 127, 2) * not_last
            both = jnp.where(lane3 == 0, up, down)
            main = both[1:9].reshape(128, 128).T
            side = jnp.concatenate([both[0], both[9]], axis=0)
            side = jnp.concatenate([side, jnp.zeros((96, 128), F32)], axis=0).T
            for s, r in ((0, 0), (1, 127)):
                opacks[k, s, 0, pl.ds(xo, 1)] = main[r : r + 1]
                opacks[k, s, 1, pl.ds(xo, 1)] = side[r : r + 1]
            return 0
        lax.fori_loop(0, BX + 2, plane_body, 0)

    def add_halo(k):
        total = jnp.zeros((8, 128), F32)
        for iy in range(2):
            base = 4 if iy == 0 else 0
            in_y = low_y if iy == 0 else top_y
            for ix in range(3):
                part = jnp.zeros((8, 128), F32)
                for iz in range(3):
                    if iz == 1:
                        t = rpacks[k, iy, ix, iz, 0]
                    else:
                        t = pltpu.roll(rpacks[k, iy, ix, iz, 1], 112, 1)
                        t = jnp.where(lane < 16 if iz == 0 else lane >= 112, t, 0.0)
                    part = part + t * (in_y * in_x[ix] * in_z[iz])
                if ix == 1:
                    part = jnp.where(lax.div(sub, 4) == base // 4, pltpu.roll(part, 3 if iy == 0 else 7, 0), 0.0)
                else:
                    row = base if ix == 0 else base + 3
                    part = jnp.where(sub == row, pltpu.roll(part, 7 if iy == 0 else 3, 0), 0.0)
                total = total + part
        place(total, 1)

        def body(x, _):
            carried[x] = carried[x] + outs[k, x + 1, pl.ds(1, BZ)] + placed[x * 3].reshape(BZ, CH, BY)
            return 0
        lax.fori_loop(0, BX, body, 0)
        for ix in range(2):
            x = 0 if ix == 0 else BX - 1
            m = low_x if ix == 0 else top_x
            carried[x] = carried[x] + rx[k, ix] * m
            for iz in range(2):
                z = 0 if iz == 0 else BZ - 1
                carried[x, z] = carried[x, z] + rc[k, ix, iz] * (m * (low_z if iz == 0 else top_z))
        for iz in range(2):
            z = 0 if iz == 0 else BZ - 1
            m = low_z if iz == 0 else top_z
            carried[:, z] = carried[:, z] + rz[k, :, iz] * m

    def weight_grads(k):
        def body(x, acc):
            g1, g2 = acc
            g1 = g1 + dot_nt(percs[k, x, 0:112], dzs[x, 0:128])
            g2 = g2 + dot_nt(dus[x, 0:32], hids[k, x, 0:144])
            return g1, g2
        return lax.fori_loop(0, BX, body, (jnp.zeros((112, 128), F32), jnp.zeros((32, 144), F32)))

    for c in first:
        c.wait_recv()
    clear_outside(0)
    filter_columns(0)
    forward(0)
    pack_state(1)
    second = state_copies(1)
    for c in second:
        c.start()
    for c in second:
        c.wait_recv()
    clear_outside(1)
    filter_columns(1)
    forward(1)
    cells(1)
    adjoint(1)
    third = out_copies(1)
    for c in third:
        c.start()
    ga1, ga2 = weight_grads(1)
    for c in third:
        c.wait_recv()
    add_halo(1)
    cells(0)
    gb1, gb2 = weight_grads(0)
    g1, g2 = ga1 + gb1, ga2 + gb2

    both = g1[0:48] + g1[48:96]
    both = both + pltpu.roll(both, 64, 1)
    bias1 = g1[96:104]
    bias1 = bias1 + pltpu.roll(bias1, 64, 1)
    second_w = g2[0:16] + g2[16:32]
    bias2 = second_w[:, 128:129]
    second_w = second_w[:, 0:128]
    second_w = second_w + pltpu.roll(second_w, 64, 1)
    left = lax.broadcasted_iota(jnp.int32, (16, 128), 1) < 64
    both = both * 0.125
    sums[0:16] = jnp.where(left, both[0:16], second_w)
    sums[16:24] = jnp.where(left[0:8], both[16:24], bias1)
    sums[24:40] = jnp.where(left, both[24:40], jnp.broadcast_to(bias2, (16, 128)))
    sums[40:48] = both[40:48]

    pieces = ny * nz
    rows = 48 // pieces
    for p in range(pieces):
        src1[p, 0:rows] = sums[p * rows : (p + 1) * rows]
    mine = gy * nz + gz

    def member(o):
        _, y, z = device(o)
        return y * nz + z

    stage1 = [pltpu.make_async_remote_copy(
        src_ref=src1.at[member(o)], dst_ref=rx1.at[i],
        send_sem=ar_send.at[0, i], recv_sem=ar_recv.at[0, i],
        device_id=device(o), device_id_type=MESH) for i, o in enumerate(plane)]
    for c in stage1:
        c.start()
    adjoint(0)
    fourth = out_copies(0)
    for c in fourth:
        c.start()
    total = src1[mine]
    for i, c in enumerate(stage1):
        c.wait_recv()
        total = total + rx1[i]
    rx2[gx] = total
    stage2 = [pltpu.make_async_remote_copy(
        src_ref=rx2.at[gx], dst_ref=rx2.at[gx],
        send_sem=ar_send.at[1, i], recv_sem=ar_recv.at[1, i],
        device_id=device(o), device_id_type=MESH) for i, o in enumerate(line)]
    for c in stage2:
        c.start()
    for c in fourth:
        c.wait_recv()
    add_halo(0)
    for x in range(BX):
        for z in range(BZ):
            grad_ref[pl.ds(x * BZ + z, CH, stride=BX * BZ), :] = carried[x, z]
    for c in stage2:
        c.wait_recv()
    for c in stage2:
        c.wait_send()
    total = rx2[0]
    for i in range(1, nx):
        total = total + rx2[i]
    rx3[mine] = total
    stage3 = [pltpu.make_async_remote_copy(
        src_ref=rx3.at[mine], dst_ref=rx3.at[mine],
        send_sem=ar_send.at[2, i], recv_sem=ar_recv.at[2, i],
        device_id=device(o), device_id_type=MESH) for i, o in enumerate(plane)]
    for c in stage3:
        c.start()
    for c in first + second + third + fourth + stage1:
        c.wait_send()
    for c in stage3:
        c.wait_recv()
    for p in range(pieces):
        sums[p * rows : (p + 1) * rows] = rx3[p, 0:rows]
    scale = 1.0 / math.sqrt(nx * BX * ny * BY * nz * BZ)
    final = sums[...] * scale
    gw1_ref[...] = final[:, 0:64]
    gb1_ref[...] = final[16:17, 64:128]
    turn[0:48] = final
    turned = turn[...].T
    gw2_ref[...] = turned[64:128, 0:16]
    gb2_ref[...] = turned[64:65, 24:40]
    for c in stage3:
        c.wait_send()


def body(start_state, cotangent, update_masks, first_weight, first_bias, second_weight, second_bias):
    sizes = (lax.axis_size("gx"), lax.axis_size("gy"), lax.axis_size("gz"))
    pieces = sizes[1] * sizes[2]
    vmem = pl.BlockSpec(memory_space=pltpu.VMEM)
    scratch = [
        pltpu.VMEM((2, BX + 2, BZ + 2, CH, BY), F32),
        pltpu.VMEM((2, 8, 128), F32),
        pltpu.VMEM((2, 2, 3, 3, 8, 128), F32),
        pltpu.VMEM((2, BX + 2, BZ + 2, CH, BY), F32),
        pltpu.VMEM((2, 2, 2, 8, 128), F32),
        pltpu.VMEM((2, 2, BZ, CH, BY), F32),
        pltpu.VMEM((2, BX, 2, CH, BY), F32),
        pltpu.VMEM((2, 2, 2, CH, BY), F32),
        pltpu.VMEM((2, 2, 3, 3, 2, 8, 128), F32),
        pltpu.VMEM((2, BX, P_ROWS, ROW), BF16),
        pltpu.VMEM((2, BX, H_ROWS, ROW), BF16),
        pltpu.VMEM((2, BX, HID, ROW), F32),
        pltpu.VMEM((BX, 3 * HID, ROW), BF16),
        pltpu.VMEM((BX, 3 * CH, ROW), BF16),
        pltpu.VMEM((BX, BZ, CH, BY), F32),
        pltpu.VMEM((BX + 4, 3, BZ + 2, CH, BY), F32),
        pltpu.VMEM((12, 128, 128), F32),
        pltpu.VMEM((12, 128, 128), BF16),
        pltpu.VMEM((256, 128), F32),
        pltpu.VMEM((HID, P_ROWS), BF16),
        pltpu.VMEM((CH, H_ROWS), BF16),
        pltpu.VMEM((HID, 3 * CH), BF16),
        pltpu.VMEM((PERC, 3 * HID), BF16),
        pltpu.VMEM((128, 128), F32),
        pltpu.VMEM((48, 128), F32),
        pltpu.VMEM((pieces, 8, 128), F32),
        pltpu.VMEM((pieces, 8, 128), F32),
        pltpu.VMEM((sizes[0], 8, 128), F32),
        pltpu.VMEM((pieces, 8, 128), F32),
        pltpu.SemaphoreType.DMA((4, 26)),
        pltpu.SemaphoreType.DMA((4, 26)),
        pltpu.SemaphoreType.DMA((3, 16)),
        pltpu.SemaphoreType.DMA((3, 16)),
    ]
    outs = pl.pallas_call(
        functools.partial(kernel, sizes),
        out_shape=(
            jax.ShapeDtypeStruct((CH * BX * BZ, BY), F32),
            jax.ShapeDtypeStruct((PERC, HID), F32),
            jax.ShapeDtypeStruct((1, HID), F32),
            jax.ShapeDtypeStruct((HID, CH), F32),
            jax.ShapeDtypeStruct((1, CH), F32),
        ),
        in_specs=[vmem] * 7,
        out_specs=(vmem,) * 5,
        scratch_shapes=scratch,
        compiler_params=pltpu.CompilerParams(
            collective_id=0, has_side_effects=True, vmem_limit_bytes=40 * 1024 * 1024),
        cost_estimate=pl.CostEstimate(flops=2 * 10**8, bytes_accessed=10**6, transcendentals=524288),
        name="automaton",
    )(
        start_state.reshape(CH * BX * BZ, BY),
        cotangent.reshape(CH * BX * BZ, BY),
        update_masks.reshape(2 * BX * BZ, BY),
        first_weight, first_bias.reshape(1, HID), second_weight, second_bias.reshape(1, CH),
    )
    grad, gw1, gb1, gw2, gb2 = outs
    return grad.reshape(CH, BX, BZ, BY), gw1, gb1.reshape(HID), gw2, gb2.reshape(CH)


def solution(mesh):
    grid = P(None, "gx", "gz", "gy")
    return jax.shard_map(
        body, mesh=mesh,
        in_specs=(grid, grid, grid, P(), P(), P(), P()),
        out_specs=(grid, P(), P(), P(), P()),
        check_vma=False)
```

```python
import functools
import math

import jax
import jax.numpy as jnp
from jax import lax
from jax.experimental import pallas as pl
from jax.experimental.pallas import tpu as pltpu
from jax.sharding import PartitionSpec as P

MESH = pl.DeviceIdType.MESH
F32 = jnp.float32
BF16 = jnp.bfloat16

CH, HID, PERC = 16, 64, 48
BX, BZ, BY = 4, 8, 128
ROW = BZ * BY

P_ROWS = 2 * PERC + 16 + PERC
H_ROWS = 2 * HID + 16 + HID

DIRS = [(dx, dy, dz) for dx in (-1, 0, 1) for dy in (-1, 0, 1) for dz in (-1, 0, 1) if (dx, dy, dz) != (0, 0, 0)]
FLAT = [d for d in DIRS if d[1] == 0]
TALL = [d for d in DIRS if d[1] != 0]

FORTH = 2 * BZ * CH + 2 * BX * CH + 4 * CH + 18 * 8
BACK = 2 * BZ * CH + 2 * BX * CH + 4 * CH + 18 * 16


def high(value):
    return value.astype(BF16).astype(F32)


def split3(value):
    first = high(value)
    second = high(value - first)
    return first, second, value - first - second


def span(step, length, kind):
    if step == 0:
        return pl.ds(1, length)
    if kind == "own":
        return pl.ds(1 if step < 0 else length, 1)
    return pl.ds(0 if step < 0 else length + 1, 1)


def dot(a, b):
    return lax.dot_general(a, b, (((1,), (0,)), ((), ())), preferred_element_type=F32)


def dot_nt(a, b):
    return lax.dot_general(a, b, (((1,), (1,)), ((), ())), preferred_element_type=F32)


def kernel(
    sizes,
    state_in, cot_in, mask_in, w1_in, b1_in, w2_in, b2_in,
    grad_out, gw1_out, gb1_out, gw2_out, gb2_out,
    grad_ref, gw1_ref, gb1_ref, gw2_ref, gb2_ref,
    state_ref, cot_ref, mask_ref, w1_ref, b1_ref, w2_ref, b2_ref,
    field, packs, halos, outs, opacks, rx, rz, rc, rpacks,
    percs, hids, hidden, grads, carried, zf, placed, onehot,
    tall, l1, l2, l3, l4, turn, sums, src1, rx1, rx2, rx3,
    tally, load_sem, store_sem, send_sem, recv_sem, ar_send, ar_recv,
):
    nx, ny, nz = sizes
    loads = [pltpu.make_async_copy(a, b, load_sem.at[i]) for i, (a, b) in enumerate((
        (state_in, state_ref), (w1_in, w1_ref), (b1_in, b1_ref), (w2_in, w2_ref), (b2_in, b2_ref), (cot_in, cot_ref), (mask_in, mask_ref)))]
    for c in loads:
        c.start()
    gx, gy, gz = lax.axis_index("gx"), lax.axis_index("gy"), lax.axis_index("gz")

    def device(offset):
        ox, oy, oz = offset
        return (
            lax.rem(gx + (ox % nx), nx) if ox % nx else gx,
            lax.rem(gy + (oy % ny), ny) if oy % ny else gy,
            lax.rem(gz + (oz % nz), nz) if oz % nz else gz,
        )

    plane = [(0, a, b) for a in range(ny) for b in range(nz) if (a, b) != (0, 0)]
    line = [(a, 0, 0) for a in range(1, nx)]
    partners = []
    for o in DIRS + plane + line:
        o = (o[0] % nx, o[1] % ny, o[2] % nz)
        if o not in partners:
            partners.append(o)

    barrier = pltpu.get_barrier_semaphore()
    for o in partners:
        pl.semaphore_signal(barrier, inc=1, device_id=device(o), device_id_type=MESH)

    lane = lax.broadcasted_iota(jnp.int32, (8, 128), 1)
    sub = lax.broadcasted_iota(jnp.int32, (8, 128), 0)
    lane3 = lax.broadcasted_iota(jnp.int32, (1, 1, 128), 2)
    not_first = (lane3 > 0).astype(F32)
    not_last = (lane3 < 127).astype(F32)

    def wait_rows(rows, sem):
        pltpu.make_async_copy(tally.at[pl.ds(0, rows)], tally.at[pl.ds(0, rows)], sem).wait()

    def pack_state(k):
        def body(x, _):
            tile = field[k, x + 1, pl.ds(1, BZ)].reshape(128, 128)
            turned = tile.T
            packs[k, pl.ds(x, 1), :] = turned[0:1, :]
            packs[k, pl.ds(x + 4, 1), :] = turned[127:128, :]
            return 0
        lax.fori_loop(0, BX, body, 0)

    loads[0].wait()
    for x in range(BX):
        for z in range(BZ):
            field[0, x + 1, z + 1] = state_ref[pl.ds(x * BZ + z, CH, stride=BX * BZ), :]
    pack_state(0)

    def state_copies(k):
        copies = []
        for d in FLAT:
            copies.append(pltpu.make_async_remote_copy(
                src_ref=field.at[k, span(d[0], BX, "own"), span(d[2], BZ, "own")],
                dst_ref=field.at[k, span(-d[0], BX, "halo"), span(-d[2], BZ, "halo")],
                send_sem=send_sem.at[k], recv_sem=recv_sem.at[k],
                device_id=device(d), device_id_type=MESH))
        for d in TALL:
            copies.append(pltpu.make_async_remote_copy(
                src_ref=packs.at[k],
                dst_ref=halos.at[k, 0 if d[1] > 0 else 1, 1 - d[0], 1 - d[2]],
                send_sem=send_sem.at[k], recv_sem=recv_sem.at[k],
                device_id=device(d), device_id_type=MESH))
        return copies

    def out_copies(k):
        copies = []
        for d in FLAT:
            if d[0] and d[2]:
                dst = rc.at[k, pl.ds(0 if d[0] > 0 else 1, 1), pl.ds(0 if d[2] > 0 else 1, 1)]
            elif d[0]:
                dst = rx.at[k, pl.ds(0 if d[0] > 0 else 1, 1)]
            else:
                dst = rz.at[k, :, pl.ds(0 if d[2] > 0 else 1, 1)]
            copies.append(pltpu.make_async_remote_copy(
                src_ref=outs.at[k, span(d[0], BX, "halo"), span(d[2], BZ, "halo")],
                dst_ref=dst,
                send_sem=send_sem.at[2 + k], recv_sem=recv_sem.at[2 + k],
                device_id=device(d), device_id_type=MESH))
        for d in TALL:
            copies.append(pltpu.make_async_remote_copy(
                src_ref=opacks.at[k, 0 if d[1] < 0 else 1],
                dst_ref=rpacks.at[k, 0 if d[1] > 0 else 1, 1 - d[0], 1 - d[2]],
                send_sem=send_sem.at[2 + k], recv_sem=recv_sem.at[2 + k],
                device_id=device(d), device_id_type=MESH))
        return copies

    pl.semaphore_wait(barrier, len(partners))
    first = state_copies(0)
    for c in first:
        c.start()

    for c in loads[1:5]:
        c.wait()
    tall[...] = jnp.zeros_like(tall)
    w1 = w1_ref[...] * 0.125
    w1h = high(w1)
    tall[0:48, 0:64] = w1h
    tall[48:96, 0:64] = w1h
    b1 = split3(b1_ref[...])
    for s in range(3):
        tall[96 + s : 97 + s, 0:64] = b1[s]
    tall[112:160, 0:64] = w1 - w1h
    l1[...] = tall[...].T[0:64, 0:P_ROWS].astype(BF16)

    tall[...] = jnp.zeros_like(tall)
    w2t = w2_ref[...]
    tall[0:16, 0:64] = w2t
    w2 = tall[...].T[0:64, 0:16]
    tall[...] = jnp.zeros_like(tall)
    w2h = high(w2)
    tall[0:64, 0:16] = w2h
    tall[64:128, 0:16] = w2h
    b2 = split3(b2_ref[...])
    for s in range(3):
        tall[128 + s : 129 + s, 0:16] = b2[s]
    tall[144:208, 0:16] = w2 - w2h
    l2[...] = tall[...].T[0:16, 0:H_ROWS].astype(BF16)

    tall[...] = jnp.zeros_like(tall)
    tall[0:48, 0:64] = -w1
    w1t = tall[...].T[0:64, 0:48]
    tall[...] = jnp.zeros_like(tall)
    w1th = high(w1t)
    tall[0:64, 0:48] = w1t - w1th
    tall[64:128, 0:48] = w1th
    tall[128:192, 0:48] = w1th
    l4[...] = tall[...].T[0:48, 0:192].astype(BF16)

    tall[...] = jnp.zeros_like(tall)
    w2th = high(w2t)
    tall[0:16, 0:64] = w2th
    tall[16:32, 0:64] = w2th
    tall[32:48, 0:64] = w2t - w2th
    l3[...] = tall[...].T[0:64, 0:48].astype(BF16)

    kk = lax.broadcasted_iota(jnp.int32, (128, 128), 0)
    yy = lax.broadcasted_iota(jnp.int32, (128, 128), 1)
    feature = lax.rem(lax.div(kk, 8), 3)
    row8 = lax.rem(kk, 8)
    hit = jnp.logical_and(kk < 72, yy == jnp.where(row8 < 4, 127, 0))
    for x in range(BX):
        for f in range(3):
            sign = jnp.where(row8 < 4, 1.0, -1.0) if f == 1 else 1.0
            onehot[x * 3 + f] = jnp.where(
                jnp.logical_and(hit, jnp.logical_and(feature == f, lax.rem(row8, 4) == x)), sign, 0.0
            ).astype(BF16)
    turn[...] = jnp.zeros_like(turn)
    for k in range(2):
        for x in range(BX):
            percs[k, x, 2 * PERC : 2 * PERC + 16, :] = jnp.ones((16, ROW), BF16)
            hids[k, x, 2 * HID : 2 * HID + 16, :] = jnp.ones((16, ROW), BF16)
    for x in (0, 1, BX + 2, BX + 3):
        zf[x] = jnp.zeros_like(zf[x])
    for c in loads[5:]:
        c.wait()
    for x in range(BX):
        for z in range(BZ):
            carried[x, z] = cot_ref[pl.ds(x * BZ + z, CH, stride=BX * BZ), :]

    low_x, top_x = (gx > 0).astype(F32), (gx < nx - 1).astype(F32)
    low_y, top_y = (gy > 0).astype(F32), (gy < ny - 1).astype(F32)
    low_z, top_z = (gz > 0).astype(F32), (gz < nz - 1).astype(F32)
    in_x, in_z = (low_x, 1.0, top_x), (low_z, 1.0, top_z)

    def halves(value):
        hi = value.astype(BF16)
        return hi, (value - hi.astype(F32)).astype(BF16)

    def place(rows24, features):
        parts = split3(rows24)
        n = 8 * features
        for s in range(3):
            turn[24 * s : 24 * s + n, :] = parts[s]
        turned = turn[...].T.astype(BF16)
        for x in range(BX):
            for f in range(features):
                placed[x * 3 + f] = dot(turned, onehot[x * 3 + f])

    def clear_outside(k):
        @pl.when(gx == 0)
        def _():
            field[k, 0] = jnp.zeros_like(field[k, 0])
        @pl.when(gx == nx - 1)
        def _():
            field[k, BX + 1] = jnp.zeros_like(field[k, BX + 1])
        @pl.when(gz == 0)
        def _():
            field[k, :, 0] = jnp.zeros_like(field[k, :, 0])
        @pl.when(gz == nz - 1)
        def _():
            field[k, :, BZ + 1] = jnp.zeros_like(field[k, :, BZ + 1])

    def filter_columns(k):
        grid = {}
        for ix in range(3):
            for iz in range(3):
                tile = jnp.where(sub < 4, halos[k, 1, ix, iz] * top_y, halos[k, 0, ix, iz] * low_y)
                grid[ix, iz] = tile * (in_x[ix] * in_z[iz])
        xs, xd = [], []
        for iz in range(3):
            mid = grid[1, iz]
            after = pltpu.roll(jnp.where(lax.rem(sub, 4) == 0, pltpu.roll(grid[2, iz], 4, 0), mid), 7, 0)
            before = pltpu.roll(jnp.where(lax.rem(sub, 4) == 3, pltpu.roll(grid[0, iz], 4, 0), mid), 1, 0)
            xs.append(before + 2.0 * mid + after)
            xd.append(after - before)

        def around(t):
            above = pltpu.roll(jnp.where(lane < 16, t[2], t[1]), 112, 1)
            below = pltpu.roll(jnp.where(lane >= 112, t[0], t[1]), 16, 1)
            return below, above

        d_below, d_above = around(xd)
        s_below, s_above = around(xs)
        place(jnp.concatenate([
            d_below + 2.0 * xd[1] + d_above,
            s_below + 2.0 * xs[1] + s_above,
            s_above - s_below], axis=0), 3)

    def forward(k):
        def body(x, _):
            zs, zd = [], []
            for i in range(3):
                v = field[k, x + i]
                zs.append(v[0:8] + 2.0 * v[1:9] + v[2:10])
                zd.append(v[2:10] - v[0:8])
            b = zs[2] - zs[0]
            a = zs[0] + 2.0 * zs[1] + zs[2]
            c = zd[0] + 2.0 * zd[1] + zd[2]
            up = lambda t: pltpu.roll(t, 127, 2) * not_last
            down = lambda t: pltpu.roll(t, 1, 2) * not_first
            features = (
                2.0 * b + up(b) + down(b),
                up(a) - down(a),
                2.0 * c + up(c) + down(c),
            )
            for f in range(3):
                perc = features[f] + placed[x * 3 + f].reshape(BZ, CH, BY)
                flat = jnp.concatenate([perc[z] for z in range(BZ)], axis=1)
                hi, lo = halves(flat)
                percs[k, x, f * 16 : f * 16 + 16] = hi
                percs[k, x, 48 + f * 16 : 64 + f * 16] = lo
                percs[k, x, 112 + f * 16 : 128 + f * 16] = hi
            hid = jnp.tanh(dot(l1[...], percs[k, x]))
            hidden[k, x] = hid
            hi, lo = halves(hid)
            hids[k, x, 0:64] = hi
            hids[k, x, 64:128] = lo
            hids[k, x, 144:208] = hi
            if k == 0:
                update = dot(l2[...], hids[k, x])
                mask = mask_ref[pl.ds(pl.multiple_of(x * BZ, 8), BZ), :].astype(F32)
                for z in range(BZ):
                    field[1, x + 1, z + 1] = field[0, x + 1, z + 1] + mask[z : z + 1] * update[:, z * BY : (z + 1) * BY]
            return 0
        lax.fori_loop(0, BX, body, 0)

    def cells(k):
        def body(x, _):
            mask = mask_ref[pl.ds(pl.multiple_of((k * BX + x) * BZ, 8), BZ), :].astype(F32)
            g = carried[x]
            du = jnp.concatenate([mask[z : z + 1] * g[z] for z in range(BZ)], axis=1)
            hi, lo = halves(du)
            grads[x, 192:208] = hi
            grads[x, 208:224] = lo
            grads[x, 224:240] = hi
            hid = hidden[k, x]
            dz = dot(l3[...], grads[x, 192:240]) * (1.0 - hid * hid)
            hi, lo = halves(dz)
            grads[x, 0:64] = hi
            grads[x, 64:128] = hi
            grads[x, 128:192] = lo
            return 0
        lax.fori_loop(0, BX, body, 0)

    def adjoint(k):
        def body(x, _):
            dp = dot(l4[...], grads[x, 0:192])
            zero = jnp.zeros((2, CH, BY), F32)
            for f in range(3):
                q = jnp.concatenate(
                    [zero] + [dp[f * 16 : f * 16 + 16, z * BY : (z + 1) * BY].reshape(1, CH, BY) for z in range(BZ)] + [zero], axis=0)
                zf[x + 2, f] = q[2:12] - q[0:10] if f == 2 else q[0:10] + 2.0 * q[1:11] + q[2:12]
            return 0
        lax.fori_loop(0, BX, body, 0)

        def plane_body(xo, _):
            pr = zf[xo + 2, 0] - zf[xo, 0] + zf[xo, 2] + 2.0 * zf[xo + 1, 2] + zf[xo + 2, 2]
            q = zf[xo, 1] + 2.0 * zf[xo + 1, 1] + zf[xo + 2, 1]
            up, down = pr + q, pr - q
            outs[k, xo] = 2.0 * pr + pltpu.roll(down, 1, 2) * not_first + pltpu.roll(up, 127, 2) * not_last
            both = jnp.where(lane3 == 0, up, down)
            main = both[1:9].reshape(128, 128).T
            side = jnp.concatenate([both[0], both[9]], axis=0)
            side = jnp.concatenate([side, jnp.zeros((96, 128), F32)], axis=0).T
            for s, r in ((0, 0), (1, 127)):
                opacks[k, s, 0, pl.ds(xo, 1)] = main[r : r + 1]
                opacks[k, s, 1, pl.ds(xo, 1)] = side[r : r + 1]
            return 0
        lax.fori_loop(0, BX + 2, plane_body, 0)

    def add_halo(k):
        total = jnp.zeros((8, 128), F32)
        for iy in range(2):
            base = 4 if iy == 0 else 0
            in_y = low_y if iy == 0 else top_y
            for ix in range(3):
                part = jnp.zeros((8, 128), F32)
                for iz in range(3):
                    if iz == 1:
                        t = rpacks[k, iy, ix, iz, 0]
                    else:
                        t = pltpu.roll(rpacks[k, iy, ix, iz, 1], 112, 1)
                        t = jnp.where(lane < 16 if iz == 0 else lane >= 112, t, 0.0)
                    part = part + t * (in_y * in_x[ix] * in_z[iz])
                if ix == 1:
                    part = jnp.where(lax.div(sub, 4) == base // 4, pltpu.roll(part, 3 if iy == 0 else 7, 0), 0.0)
                else:
                    row = base if ix == 0 else base + 3
                    part = jnp.where(sub == row, pltpu.roll(part, 7 if iy == 0 else 3, 0), 0.0)
                total = total + part
        place(total, 1)

        def body(x, _):
            carried[x] = carried[x] + outs[k, x + 1, pl.ds(1, BZ)] + placed[x * 3].reshape(BZ, CH, BY)
            return 0
        lax.fori_loop(0, BX, body, 0)
        for ix in range(2):
            x = 0 if ix == 0 else BX - 1
            m = low_x if ix == 0 else top_x
            carried[x] = carried[x] + rx[k, ix] * m
            for iz in range(2):
                z = 0 if iz == 0 else BZ - 1
                carried[x, z] = carried[x, z] + rc[k, ix, iz] * (m * (low_z if iz == 0 else top_z))
        for iz in range(2):
            z = 0 if iz == 0 else BZ - 1
            m = low_z if iz == 0 else top_z
            carried[:, z] = carried[:, z] + rz[k, :, iz] * m

    def weight_grads(k):
        def body(x, acc):
            g1, g2 = acc
            g1 = g1 + dot_nt(percs[k, x, 0:112], grads[x, 64:224])
            g2 = g2 + dot_nt(grads[x, 192:224], hids[k, x, 0:128])
            return g1, g2
        return lax.fori_loop(0, BX, body, (jnp.zeros((112, 160), F32), jnp.zeros((32, 128), F32)))

    wait_rows(FORTH, recv_sem.at[0])
    clear_outside(0)
    filter_columns(0)
    forward(0)
    pack_state(1)
    for c in state_copies(1):
        c.start()
    wait_rows(FORTH, send_sem.at[0])
    wait_rows(FORTH, recv_sem.at[1])
    clear_outside(1)
    filter_columns(1)
    forward(1)
    cells(1)
    adjoint(1)
    for c in out_copies(1):
        c.start()
    ga1, ga2 = weight_grads(1)
    wait_rows(FORTH, send_sem.at[1])
    wait_rows(BACK, recv_sem.at[3])
    add_halo(1)
    cells(0)
    gb1, gb2 = weight_grads(0)
    g1, g2 = ga1 + gb1, ga2 + gb2

    both = (g1[0:48] + g1[48:96])[:, 0:128]
    both = (both + pltpu.roll(both, 64, 1)) * 0.125
    bias1 = g1[96:104, 0:128]
    bias1 = bias1 + pltpu.roll(bias1, 64, 1)
    bias2 = jnp.concatenate([g1[96:104, 128:160], jnp.zeros((8, 96), F32)], axis=1)
    bias2 = pltpu.roll(bias2, 64, 1) + pltpu.roll(bias2, 48, 1)
    second_w = g2[0:16] + g2[16:32]
    second_w = second_w + pltpu.roll(second_w, 64, 1)
    left = lax.broadcasted_iota(jnp.int32, (16, 128), 1) < 64
    sums[0:16] = jnp.where(left, both[0:16], second_w)
    sums[16:24] = jnp.where(left[0:8], both[16:24], bias1)
    sums[24:32] = jnp.where(left[0:8], both[24:32], bias2)
    sums[32:48] = both[32:48]

    pieces = ny * nz
    rows = 48 // pieces
    for p in range(pieces):
        src1[p, 0:rows] = sums[p * rows : (p + 1) * rows]
    mine = gy * nz + gz

    def member(o):
        _, y, z = device(o)
        return y * nz + z

    stage1 = [pltpu.make_async_remote_copy(
        src_ref=src1.at[member(o)], dst_ref=rx1.at[i],
        send_sem=ar_send.at[0], recv_sem=ar_recv.at[0],
        device_id=device(o), device_id_type=MESH) for i, o in enumerate(plane)]
    for c in stage1:
        c.start()
    adjoint(0)
    for c in out_copies(0):
        c.start()
    wait_rows(8 * len(plane), ar_recv.at[0])
    total = src1[mine]
    for i in range(len(plane)):
        total = total + rx1[i]
    rx2[gx] = total
    stage2 = [pltpu.make_async_remote_copy(
        src_ref=rx2.at[gx], dst_ref=rx2.at[gx],
        send_sem=ar_send.at[1], recv_sem=ar_recv.at[1],
        device_id=device(o), device_id_type=MESH) for o in line]
    for c in stage2:
        c.start()
    wait_rows(BACK, send_sem.at[3])
    wait_rows(8 * len(plane), ar_send.at[0])
    wait_rows(BACK, recv_sem.at[2])
    add_halo(0)
    for x in range(BX):
        for z in range(BZ):
            grad_ref[pl.ds(x * BZ + z, CH, stride=BX * BZ), :] = carried[x, z]
    stores = [pltpu.make_async_copy(a, b, store_sem.at[i]) for i, (a, b) in enumerate((
        (grad_ref, grad_out), (gw1_ref, gw1_out), (gb1_ref, gb1_out), (gw2_ref, gw2_out), (gb2_ref, gb2_out)))]
    stores[0].start()
    wait_rows(8 * len(line), ar_recv.at[1])
    wait_rows(8 * len(line), ar_send.at[1])
    total = rx2[0]
    for i in range(1, nx):
        total = total + rx2[i]
    rx3[mine] = total
    stage3 = [pltpu.make_async_remote_copy(
        src_ref=rx3.at[mine], dst_ref=rx3.at[mine],
        send_sem=ar_send.at[2], recv_sem=ar_recv.at[2],
        device_id=device(o), device_id_type=MESH) for o in plane]
    for c in stage3:
        c.start()
    wait_rows(BACK, send_sem.at[2])
    wait_rows(8 * len(plane), ar_send.at[2])
    wait_rows(8 * len(plane), ar_recv.at[2])
    for p in range(pieces):
        sums[p * rows : (p + 1) * rows] = rx3[p, 0:rows]
    scale = 1.0 / math.sqrt(nx * BX * ny * BY * nz * BZ)
    final = sums[...] * scale
    gw1_ref[...] = final[:, 0:64]
    gb1_ref[...] = final[16:17, 64:128]
    gw2_ref[...] = final[0:16, 64:128]
    gb2_ref[...] = final[24:25, 64:80]
    for c in stores[1:]:
        c.start()
    for c in stores:
        c.wait()


def write_out(*refs):
    sems = refs[-1]
    copies = [pltpu.make_async_copy(refs[i], refs[5 + i], sems.at[i]) for i in range(5)]
    for c in copies:
        c.start()
    for c in copies:
        c.wait()


def body(start_state, cotangent, update_masks, first_weight, first_bias, second_weight, second_bias):
    sizes = (lax.axis_size("gx"), lax.axis_size("gy"), lax.axis_size("gz"))
    pieces = sizes[1] * sizes[2]
    hbm = pl.BlockSpec(memory_space=pltpu.HBM)
    shapes = ((CH * BX * BZ, BY), (PERC, HID), (1, HID), (CH, HID), (1, CH))
    shapes = tuple(jax.ShapeDtypeStruct(s, F32) for s in shapes)
    scratch = [
        pltpu.VMEM((CH * BX * BZ, BY), F32),
        pltpu.VMEM((PERC, HID), F32),
        pltpu.VMEM((1, HID), F32),
        pltpu.VMEM((CH, HID), F32),
        pltpu.VMEM((1, CH), F32),
        pltpu.VMEM((CH * BX * BZ, BY), F32),
        pltpu.VMEM((CH * BX * BZ, BY), F32),
        pltpu.VMEM((2 * BX * BZ, BY), jnp.int32),
        pltpu.VMEM((PERC, HID), F32),
        pltpu.VMEM((1, HID), F32),
        pltpu.VMEM((CH, HID), F32),
        pltpu.VMEM((1, CH), F32),
        pltpu.VMEM((2, BX + 2, BZ + 2, CH, BY), F32),
        pltpu.VMEM((2, 8, 128), F32),
        pltpu.VMEM((2, 2, 3, 3, 8, 128), F32),
        pltpu.VMEM((2, BX + 2, BZ + 2, CH, BY), F32),
        pltpu.VMEM((2, 2, 2, 8, 128), F32),
        pltpu.VMEM((2, 2, BZ, CH, BY), F32),
        pltpu.VMEM((2, BX, 2, CH, BY), F32),
        pltpu.VMEM((2, 2, 2, CH, BY), F32),
        pltpu.VMEM((2, 2, 3, 3, 2, 8, 128), F32),
        pltpu.VMEM((2, BX, P_ROWS, ROW), BF16),
        pltpu.VMEM((2, BX, H_ROWS, ROW), BF16),
        pltpu.VMEM((2, BX, HID, ROW), F32),
        pltpu.VMEM((BX, 3 * HID + 3 * CH, ROW), BF16),
        pltpu.VMEM((BX, BZ, CH, BY), F32),
        pltpu.VMEM((BX + 4, 3, BZ + 2, CH, BY), F32),
        pltpu.VMEM((12, 128, 128), F32),
        pltpu.VMEM((12, 128, 128), BF16),
        pltpu.VMEM((256, 128), F32),
        pltpu.VMEM((HID, P_ROWS), BF16),
        pltpu.VMEM((CH, H_ROWS), BF16),
        pltpu.VMEM((HID, 3 * CH), BF16),
        pltpu.VMEM((PERC, 3 * HID), BF16),
        pltpu.VMEM((128, 128), F32),
        pltpu.VMEM((48, 128), F32),
        pltpu.VMEM((pieces, 8, 128), F32),
        pltpu.VMEM((pieces, 8, 128), F32),
        pltpu.VMEM((sizes[0], 8, 128), F32),
        pltpu.VMEM((pieces, 8, 128), F32),
        pltpu.VMEM((BACK, 128), F32),
        pltpu.SemaphoreType.DMA((7,)),
        pltpu.SemaphoreType.DMA((5,)),
        pltpu.SemaphoreType.DMA((4,)),
        pltpu.SemaphoreType.DMA((4,)),
        pltpu.SemaphoreType.DMA((3,)),
        pltpu.SemaphoreType.DMA((3,)),
    ]
    outs = pl.pallas_call(
        functools.partial(kernel, sizes),
        out_shape=shapes,
        in_specs=[hbm] * 7,
        out_specs=(hbm,) * 5,
        scratch_shapes=scratch,
        compiler_params=pltpu.CompilerParams(
            collective_id=0, has_side_effects=True, vmem_limit_bytes=60 * 1024 * 1024),
        cost_estimate=pl.CostEstimate(flops=2 * 10**8, bytes_accessed=10**6, transcendentals=524288),
        name="automaton",
    )(
        start_state.reshape(CH * BX * BZ, BY),
        cotangent.reshape(CH * BX * BZ, BY),
        update_masks.reshape(2 * BX * BZ, BY),
        first_weight, first_bias.reshape(1, HID), second_weight.T, second_bias.reshape(1, CH),
    )
    grad, gw1, gb1, gw2, gb2 = pl.pallas_call(
        write_out,
        out_shape=shapes,
        in_specs=[pl.BlockSpec(memory_space=pltpu.VMEM)] * 5,
        out_specs=(hbm,) * 5,
        scratch_shapes=[pltpu.SemaphoreType.DMA((5,))],
        cost_estimate=pl.CostEstimate(flops=0, bytes_accessed=600000, transcendentals=0),
        name="write_out",
    )(*outs)
    return grad.reshape(CH, BX, BZ, BY), gw1, gb1.reshape(HID), gw2.T, gb2.reshape(CH)


def solution(mesh):
    grid = P(None, "gx", "gz", "gy")
    return jax.shard_map(
        body, mesh=mesh,
        in_specs=(grid, grid, grid, P(), P(), P(), P()),
        out_specs=(grid, P(), P(), P(), P()),
        check_vma=False)
```

```python
import functools
import math

import jax
import jax.numpy as jnp
from jax import lax
from jax.experimental import pallas as pl
from jax.experimental.pallas import tpu as pltpu
from jax.sharding import PartitionSpec as P

MESH = pl.DeviceIdType.MESH
F32 = jnp.float32
BF16 = jnp.bfloat16

CH, HID, PERC = 16, 64, 48
BX, BZ, BY = 4, 8, 128
ROW = BZ * BY

P_ROWS = 2 * PERC + 16 + PERC
H_ROWS = 2 * HID + 16 + HID

DIRS = [(dx, dy, dz) for dx in (-1, 0, 1) for dy in (-1, 0, 1) for dz in (-1, 0, 1) if (dx, dy, dz) != (0, 0, 0)]
DIRS = sorted(DIRS, key=lambda d: -sum(map(abs, d)))

FORTH = 2 * BZ * CH + 2 * BX * CH + 4 * CH + 18 * 8
BACK = 2 * BZ * CH + 2 * BX * CH + 4 * CH + 18 * 16


def high(value):
    return value.astype(BF16).astype(F32)


def split3(value):
    first = high(value)
    second = high(value - first)
    return first, second, value - first - second


def span(step, length, kind):
    if step == 0:
        return pl.ds(1, length)
    if kind == "own":
        return pl.ds(1 if step < 0 else length, 1)
    return pl.ds(0 if step < 0 else length + 1, 1)


def dot(a, b):
    return lax.dot_general(a, b, (((1,), (0,)), ((), ())), preferred_element_type=F32)


def dot_nt(a, b):
    return lax.dot_general(a, b, (((1,), (1,)), ((), ())), preferred_element_type=F32)


def kernel(
    sizes,
    state_in, cot_in, mask_in, w1_in, b1_in, w2_in, b2_in,
    grad_out, gw1_out, gb1_out, gw2_out, gb2_out,
    grad_ref, gw1_ref, gb1_ref, gw2_ref, gb2_ref,
    state_ref, cot_ref, mask_ref, w1_ref, b1_ref, w2_ref, b2_ref,
    field, packs, halos, outs, opacks, rx, rz, rc, rpacks,
    percs, hids, hidden, grads, carried, zf, placed, onehot,
    tall, l1, l2, l3, l4, turn, sums, rx0, rx1, rx2, whole,
    tally, load_sem, store_sem, send_sem, recv_sem, ar_send, ar_recv,
):
    nx, ny, nz = sizes
    loads = [pltpu.make_async_copy(a, b, load_sem.at[i]) for i, (a, b) in enumerate((
        (state_in, state_ref), (w1_in, w1_ref), (b1_in, b1_ref), (w2_in, w2_ref), (b2_in, b2_ref), (cot_in, cot_ref), (mask_in, mask_ref)))]
    for c in loads:
        c.start()
    gx, gy, gz = lax.axis_index("gx"), lax.axis_index("gy"), lax.axis_index("gz")

    def device(offset):
        ox, oy, oz = offset
        return (
            lax.rem(gx + (ox % nx), nx) if ox % nx else gx,
            lax.rem(gy + (oy % ny), ny) if oy % ny else gy,
            lax.rem(gz + (oz % nz), nz) if oz % nz else gz,
        )

    def far(o):
        return -sum(min(a, n - a) for a, n in zip(o, sizes))

    plane = sorted(((0, a, b) for a in range(ny) for b in range(nz) if (a, b) != (0, 0)), key=far)
    line = sorted(((a, 0, 0) for a in range(2, nx, 2)), key=far)
    core = lax.rem(gx, 2)
    partners = []
    for o in DIRS + plane + line:
        o = (o[0] % nx, o[1] % ny, o[2] % nz)
        if o not in partners:
            partners.append(o)
    partners.sort(key=far)

    barrier = pltpu.get_barrier_semaphore()
    for o in partners:
        pl.semaphore_signal(barrier, inc=1, device_id=device(o), device_id_type=MESH)

    lane = lax.broadcasted_iota(jnp.int32, (8, 128), 1)
    sub = lax.broadcasted_iota(jnp.int32, (8, 128), 0)
    lane3 = lax.broadcasted_iota(jnp.int32, (1, 1, 128), 2)
    not_first = (lane3 > 0).astype(F32)
    not_last = (lane3 < 127).astype(F32)

    def wait_rows(rows, sem):
        pltpu.make_async_copy(tally.at[pl.ds(0, rows)], tally.at[pl.ds(0, rows)], sem).wait()

    def pack_state(k):
        def body(x, _):
            tile = field[k, x + 1, pl.ds(1, BZ)].reshape(128, 128)
            turned = tile.T
            packs[k, pl.ds(x, 1), :] = turned[0:1, :]
            packs[k, pl.ds(x + 4, 1), :] = turned[127:128, :]
            return 0
        lax.fori_loop(0, BX, body, 0, unroll=True)

    loads[0].wait()
    for x in range(BX):
        for z in range(BZ):
            field[0, x + 1, z + 1] = state_ref[pl.ds(x * BZ + z, CH, stride=BX * BZ), :]
    pack_state(0)

    def state_copies(k):
        copies = []
        for d in DIRS:
            if d[1]:
                src = packs.at[k]
                dst = halos.at[k, 0 if d[1] > 0 else 1, 1 - d[0], 1 - d[2]]
            else:
                src = field.at[k, span(d[0], BX, "own"), span(d[2], BZ, "own")]
                dst = field.at[k, span(-d[0], BX, "halo"), span(-d[2], BZ, "halo")]
            copies.append(pltpu.make_async_remote_copy(
                src_ref=src, dst_ref=dst, send_sem=send_sem.at[k], recv_sem=recv_sem.at[k],
                device_id=device(d), device_id_type=MESH))
        return copies

    def out_copies(k):
        copies = []
        for d in DIRS:
            at_x, at_z = pl.ds(0 if d[0] > 0 else 1, 1), pl.ds(0 if d[2] > 0 else 1, 1)
            if d[1]:
                src = opacks.at[k, 0 if d[1] < 0 else 1]
                dst = rpacks.at[k, 0 if d[1] > 0 else 1, 1 - d[0], 1 - d[2]]
            else:
                src = outs.at[k, span(d[0], BX, "halo"), span(d[2], BZ, "halo")]
                if d[0] and d[2]:
                    dst = rc.at[k, at_x, at_z]
                elif d[0]:
                    dst = rx.at[k, at_x]
                else:
                    dst = rz.at[k, :, at_z]
            copies.append(pltpu.make_async_remote_copy(
                src_ref=src, dst_ref=dst, send_sem=send_sem.at[2 + k], recv_sem=recv_sem.at[2 + k],
                device_id=device(d), device_id_type=MESH))
        return copies

    pl.semaphore_wait(barrier, len(partners))
    first = state_copies(0)
    for c in first:
        c.start()

    for c in loads[1:5]:
        c.wait()
    tall[...] = jnp.zeros_like(tall)
    w1 = w1_ref[...] * 0.125
    w1h = high(w1)
    tall[0:48, 0:64] = w1h
    tall[48:96, 0:64] = w1h
    b1 = split3(b1_ref[...])
    for s in range(3):
        tall[96 + s : 97 + s, 0:64] = b1[s]
    tall[112:160, 0:64] = w1 - w1h
    l1[...] = tall[...].T[0:64, 0:P_ROWS].astype(BF16)

    tall[...] = jnp.zeros_like(tall)
    w2t = w2_ref[...]
    tall[0:16, 0:64] = w2t
    w2 = tall[...].T[0:64, 0:16]
    tall[...] = jnp.zeros_like(tall)
    w2h = high(w2)
    tall[0:64, 0:16] = w2h
    tall[64:128, 0:16] = w2h
    b2 = split3(b2_ref[...])
    for s in range(3):
        tall[128 + s : 129 + s, 0:16] = b2[s]
    tall[144:208, 0:16] = w2 - w2h
    l2[...] = tall[...].T[0:16, 0:H_ROWS].astype(BF16)

    tall[...] = jnp.zeros_like(tall)
    tall[0:48, 0:64] = -w1
    w1t = tall[...].T[0:64, 0:48]
    tall[...] = jnp.zeros_like(tall)
    w1th = high(w1t)
    tall[0:64, 0:48] = w1t - w1th
    tall[64:128, 0:48] = w1th
    tall[128:192, 0:48] = w1th
    l4[...] = tall[...].T[0:48, 0:192].astype(BF16)

    tall[...] = jnp.zeros_like(tall)
    w2th = high(w2t)
    tall[0:16, 0:64] = w2th
    tall[16:32, 0:64] = w2th
    tall[32:48, 0:64] = w2t - w2th
    l3[...] = tall[...].T[0:64, 0:48].astype(BF16)

    kk = lax.broadcasted_iota(jnp.int32, (128, 128), 0)
    yy = lax.broadcasted_iota(jnp.int32, (128, 128), 1)
    feature = lax.rem(lax.div(kk, 8), 3)
    row8 = lax.rem(kk, 8)
    hit = jnp.logical_and(kk < 72, yy == jnp.where(row8 < 4, 127, 0))
    for x in range(BX):
        for f in range(3):
            sign = jnp.where(row8 < 4, 1.0, -1.0) if f == 1 else 1.0
            onehot[x * 3 + f] = jnp.where(
                jnp.logical_and(hit, jnp.logical_and(feature == f, lax.rem(row8, 4) == x)), sign, 0.0
            ).astype(BF16)
    turn[...] = jnp.zeros_like(turn)
    for k in range(2):
        for x in range(BX):
            percs[k, x, 2 * PERC : 2 * PERC + 16, :] = jnp.ones((16, ROW), BF16)
            hids[k, x, 2 * HID : 2 * HID + 16, :] = jnp.ones((16, ROW), BF16)
    for x in (0, 1, BX + 2, BX + 3):
        zf[x] = jnp.zeros_like(zf[x])
    for c in loads[5:]:
        c.wait()
    for x in range(BX):
        for z in range(BZ):
            carried[x, z] = cot_ref[pl.ds(x * BZ + z, CH, stride=BX * BZ), :]

    low_x, top_x = (gx > 0).astype(F32), (gx < nx - 1).astype(F32)
    low_y, top_y = (gy > 0).astype(F32), (gy < ny - 1).astype(F32)
    low_z, top_z = (gz > 0).astype(F32), (gz < nz - 1).astype(F32)
    in_x, in_z = (low_x, 1.0, top_x), (low_z, 1.0, top_z)

    def halves(value):
        hi = value.astype(BF16)
        return hi, (value - hi.astype(F32)).astype(BF16)

    def place(rows24, features):
        parts = split3(rows24)
        n = 8 * features
        for s in range(3):
            turn[24 * s : 24 * s + n, :] = parts[s]
        turned = turn[...].T.astype(BF16)
        for x in range(BX):
            for f in range(features):
                placed[x * 3 + f] = dot(turned, onehot[x * 3 + f])

    def clear_outside(k):
        @pl.when(gx == 0)
        def _():
            field[k, 0] = jnp.zeros_like(field[k, 0])
        @pl.when(gx == nx - 1)
        def _():
            field[k, BX + 1] = jnp.zeros_like(field[k, BX + 1])
        @pl.when(gz == 0)
        def _():
            field[k, :, 0] = jnp.zeros_like(field[k, :, 0])
        @pl.when(gz == nz - 1)
        def _():
            field[k, :, BZ + 1] = jnp.zeros_like(field[k, :, BZ + 1])

    def filter_columns(k):
        grid = {}
        for ix in range(3):
            for iz in range(3):
                tile = jnp.where(sub < 4, halos[k, 1, ix, iz] * top_y, halos[k, 0, ix, iz] * low_y)
                grid[ix, iz] = tile * (in_x[ix] * in_z[iz])
        xs, xd = [], []
        for iz in range(3):
            mid = grid[1, iz]
            after = pltpu.roll(jnp.where(lax.rem(sub, 4) == 0, pltpu.roll(grid[2, iz], 4, 0), mid), 7, 0)
            before = pltpu.roll(jnp.where(lax.rem(sub, 4) == 3, pltpu.roll(grid[0, iz], 4, 0), mid), 1, 0)
            xs.append(before + 2.0 * mid + after)
            xd.append(after - before)

        def around(t):
            above = pltpu.roll(jnp.where(lane < 16, t[2], t[1]), 112, 1)
            below = pltpu.roll(jnp.where(lane >= 112, t[0], t[1]), 16, 1)
            return below, above

        d_below, d_above = around(xd)
        s_below, s_above = around(xs)
        place(jnp.concatenate([
            d_below + 2.0 * xd[1] + d_above,
            s_below + 2.0 * xs[1] + s_above,
            s_above - s_below], axis=0), 3)

    def forward(k):
        def body(x, _):
            zs, zd = [], []
            for i in range(3):
                v = field[k, x + i]
                zs.append(v[0:8] + 2.0 * v[1:9] + v[2:10])
                zd.append(v[2:10] - v[0:8])
            b = zs[2] - zs[0]
            a = zs[0] + 2.0 * zs[1] + zs[2]
            c = zd[0] + 2.0 * zd[1] + zd[2]
            up = lambda t: pltpu.roll(t, 127, 2) * not_last
            down = lambda t: pltpu.roll(t, 1, 2) * not_first
            features = (
                2.0 * b + up(b) + down(b),
                up(a) - down(a),
                2.0 * c + up(c) + down(c),
            )
            for f in range(3):
                perc = features[f] + placed[x * 3 + f].reshape(BZ, CH, BY)
                flat = jnp.concatenate([perc[z] for z in range(BZ)], axis=1)
                hi, lo = halves(flat)
                percs[k, x, f * 16 : f * 16 + 16] = hi
                percs[k, x, 48 + f * 16 : 64 + f * 16] = lo
                percs[k, x, 112 + f * 16 : 128 + f * 16] = hi
            hid = jnp.tanh(dot(l1[...], percs[k, x]))
            hidden[k, x] = hid
            hi, lo = halves(hid)
            hids[k, x, 0:64] = hi
            hids[k, x, 64:128] = lo
            hids[k, x, 144:208] = hi
            if k == 0:
                update = dot(l2[...], hids[k, x])
                mask = mask_ref[pl.ds(pl.multiple_of(x * BZ, 8), BZ), :].astype(F32)
                for z in range(BZ):
                    field[1, x + 1, z + 1] = field[0, x + 1, z + 1] + mask[z : z + 1] * update[:, z * BY : (z + 1) * BY]
            return 0
        lax.fori_loop(0, BX, body, 0, unroll=True)

    def cells(k):
        def body(x, _):
            mask = mask_ref[pl.ds(pl.multiple_of((k * BX + x) * BZ, 8), BZ), :].astype(F32)
            g = carried[x]
            du = jnp.concatenate([mask[z : z + 1] * g[z] for z in range(BZ)], axis=1)
            hi, lo = halves(du)
            grads[x, 192:208] = hi
            grads[x, 208:224] = lo
            grads[x, 224:240] = hi
            hid = hidden[k, x]
            dz = dot(l3[...], grads[x, 192:240]) * (1.0 - hid * hid)
            hi, lo = halves(dz)
            grads[x, 0:64] = hi
            grads[x, 64:128] = hi
            grads[x, 128:192] = lo
            return 0
        lax.fori_loop(0, BX, body, 0, unroll=True)

    def adjoint(k):
        def body(x, _):
            dp = dot(l4[...], grads[x, 0:192])
            zero = jnp.zeros((2, CH, BY), F32)
            for f in range(3):
                q = jnp.concatenate(
                    [zero] + [dp[f * 16 : f * 16 + 16, z * BY : (z + 1) * BY].reshape(1, CH, BY) for z in range(BZ)] + [zero], axis=0)
                zf[x + 2, f] = q[2:12] - q[0:10] if f == 2 else q[0:10] + 2.0 * q[1:11] + q[2:12]
            return 0
        lax.fori_loop(0, BX, body, 0, unroll=True)

        def plane_body(xo, _):
            pr = zf[xo + 2, 0] - zf[xo, 0] + zf[xo, 2] + 2.0 * zf[xo + 1, 2] + zf[xo + 2, 2]
            q = zf[xo, 1] + 2.0 * zf[xo + 1, 1] + zf[xo + 2, 1]
            up, down = pr + q, pr - q
            outs[k, xo] = 2.0 * pr + pltpu.roll(down, 1, 2) * not_first + pltpu.roll(up, 127, 2) * not_last
            both = jnp.where(lane3 == 0, up, down)
            main = both[1:9].reshape(128, 128).T
            side = jnp.concatenate([both[0], both[9]], axis=0)
            side = jnp.concatenate([side, jnp.zeros((96, 128), F32)], axis=0).T
            for s, r in ((0, 0), (1, 127)):
                opacks[k, s, 0, pl.ds(xo, 1)] = main[r : r + 1]
                opacks[k, s, 1, pl.ds(xo, 1)] = side[r : r + 1]
            return 0
        lax.fori_loop(0, BX + 2, plane_body, 0, unroll=True)

    def add_halo(k):
        total = jnp.zeros((8, 128), F32)
        for iy in range(2):
            base = 4 if iy == 0 else 0
            in_y = low_y if iy == 0 else top_y
            for ix in range(3):
                part = jnp.zeros((8, 128), F32)
                for iz in range(3):
                    if iz == 1:
                        t = rpacks[k, iy, ix, iz, 0]
                    else:
                        t = pltpu.roll(rpacks[k, iy, ix, iz, 1], 112, 1)
                        t = jnp.where(lane < 16 if iz == 0 else lane >= 112, t, 0.0)
                    part = part + t * (in_y * in_x[ix] * in_z[iz])
                if ix == 1:
                    part = jnp.where(lax.div(sub, 4) == base // 4, pltpu.roll(part, 3 if iy == 0 else 7, 0), 0.0)
                else:
                    row = base if ix == 0 else base + 3
                    part = jnp.where(sub == row, pltpu.roll(part, 7 if iy == 0 else 3, 0), 0.0)
                total = total + part
        place(total, 1)

        def body(x, _):
            carried[x] = carried[x] + outs[k, x + 1, pl.ds(1, BZ)] + placed[x * 3].reshape(BZ, CH, BY)
            return 0
        lax.fori_loop(0, BX, body, 0, unroll=True)
        for ix in range(2):
            x = 0 if ix == 0 else BX - 1
            m = low_x if ix == 0 else top_x
            carried[x] = carried[x] + rx[k, ix] * m
            for iz in range(2):
                z = 0 if iz == 0 else BZ - 1
                carried[x, z] = carried[x, z] + rc[k, ix, iz] * (m * (low_z if iz == 0 else top_z))
        for iz in range(2):
            z = 0 if iz == 0 else BZ - 1
            m = low_z if iz == 0 else top_z
            carried[:, z] = carried[:, z] + rz[k, :, iz] * m

    def weight_grads(k):
        def body(x, acc):
            g1, g2 = acc
            g1 = g1 + dot_nt(percs[k, x, 0:112], grads[x, 64:224])
            g2 = g2 + dot_nt(grads[x, 192:224], hids[k, x, 0:128])
            return g1, g2
        return lax.fori_loop(0, BX, body, (jnp.zeros((112, 160), F32), jnp.zeros((32, 128), F32)), unroll=True)

    wait_rows(FORTH, recv_sem.at[0])
    clear_outside(0)
    filter_columns(0)
    forward(0)
    pack_state(1)
    for c in state_copies(1):
        c.start()
    wait_rows(FORTH, send_sem.at[0])
    wait_rows(FORTH, recv_sem.at[1])
    clear_outside(1)
    filter_columns(1)
    forward(1)
    cells(1)
    adjoint(1)
    for c in out_copies(1):
        c.start()
    ga1, ga2 = weight_grads(1)
    wait_rows(FORTH, send_sem.at[1])
    wait_rows(BACK, recv_sem.at[3])
    add_halo(1)
    cells(0)
    gb1, gb2 = weight_grads(0)
    g1, g2 = ga1 + gb1, ga2 + gb2

    both = (g1[0:48] + g1[48:96])[:, 0:128]
    both = (both + pltpu.roll(both, 64, 1)) * 0.125
    bias1 = g1[96:104, 0:128]
    bias1 = bias1 + pltpu.roll(bias1, 64, 1)
    bias2 = jnp.concatenate([g1[96:104, 128:160], jnp.zeros((8, 96), F32)], axis=1)
    bias2 = pltpu.roll(bias2, 64, 1) + pltpu.roll(bias2, 48, 1)
    second_w = g2[0:16] + g2[16:32]
    second_w = second_w + pltpu.roll(second_w, 64, 1)
    left = lax.broadcasted_iota(jnp.int32, (16, 128), 1) < 64
    sums[0:16] = jnp.where(left, both[0:16], second_w)
    sums[16:24] = jnp.where(left[0:8], both[16:24], bias1)
    sums[24:32] = jnp.where(left[0:8], both[24:32], bias2)
    sums[32:48] = both[32:48]

    half = sums.shape[0] // 2
    own_rows = pl.ds(pl.multiple_of(core * half, 8), half)
    other_rows = pl.ds(pl.multiple_of((1 - core) * half, 8), half)
    twin = (gx + 1 - 2 * core, gy, gz)
    mine = gy * nz + gz
    chip = lax.div(gx, 2)
    pair = pltpu.make_async_remote_copy(
        src_ref=sums.at[other_rows], dst_ref=rx0, send_sem=ar_send.at[0], recv_sem=ar_recv.at[0],
        device_id=twin, device_id_type=MESH)
    pair.start()
    pair.wait_recv()
    rx1[mine] = sums[own_rows] + rx0[...]
    stage1 = [pltpu.make_async_remote_copy(
        src_ref=rx1.at[mine], dst_ref=rx1.at[mine], send_sem=ar_send.at[1], recv_sem=ar_recv.at[1],
        device_id=device(o), device_id_type=MESH) for o in plane]
    for c in stage1:
        c.start()
    pair.wait_send()
    adjoint(0)
    for c in out_copies(0):
        c.start()
    wait_rows(half * len(plane), ar_recv.at[1])
    wait_rows(half * len(plane), ar_send.at[1])
    total = rx1[0]
    for i in range(1, ny * nz):
        total = total + rx1[i]
    rx2[chip] = total
    stage2 = [pltpu.make_async_remote_copy(
        src_ref=rx2.at[chip], dst_ref=rx2.at[chip], send_sem=ar_send.at[2], recv_sem=ar_recv.at[2],
        device_id=device(o), device_id_type=MESH) for o in line]
    for c in stage2:
        c.start()
    wait_rows(BACK, send_sem.at[3])
    wait_rows(BACK, recv_sem.at[2])
    add_halo(0)
    for x in range(BX):
        for z in range(BZ):
            grad_ref[pl.ds(x * BZ + z, CH, stride=BX * BZ), :] = carried[x, z]
    stores = [pltpu.make_async_copy(a, b, store_sem.at[i]) for i, (a, b) in enumerate((
        (grad_ref, grad_out), (gw1_ref, gw1_out), (gb1_ref, gb1_out), (gw2_ref, gw2_out), (gb2_ref, gb2_out)))]
    stores[0].start()
    wait_rows(BACK, send_sem.at[2])
    wait_rows(half * len(line), ar_recv.at[2])
    wait_rows(half * len(line), ar_send.at[2])
    total = rx2[0]
    for i in range(1, nx // 2):
        total = total + rx2[i]
    whole[own_rows] = total
    share = pltpu.make_async_remote_copy(
        src_ref=whole.at[own_rows], dst_ref=whole.at[own_rows], send_sem=ar_send.at[3], recv_sem=ar_recv.at[3],
        device_id=twin, device_id_type=MESH)
    share.start()
    share.wait()
    scale = 1.0 / math.sqrt(nx * BX * ny * BY * nz * BZ)
    final = whole[...] * scale
    gw1_ref[...] = final[:, 0:64]
    gb1_ref[...] = final[16:17, 64:128]
    gw2_ref[...] = final[0:16, 64:128]
    gb2_ref[...] = final[24:25, 64:80]
    for c in stores[1:]:
        c.start()
    for c in stores:
        c.wait()


def write_out(*refs):
    sems = refs[-1]
    copies = [pltpu.make_async_copy(refs[i], refs[5 + i], sems.at[i]) for i in range(5)]
    for c in copies:
        c.start()
    for c in copies:
        c.wait()


def body(start_state, cotangent, update_masks, first_weight, first_bias, second_weight, second_bias):
    sizes = (lax.axis_size("gx"), lax.axis_size("gy"), lax.axis_size("gz"))
    hbm = pl.BlockSpec(memory_space=pltpu.HBM)
    shapes = ((CH * BX * BZ, BY), (PERC, HID), (1, HID), (CH, HID), (1, CH))
    shapes = tuple(jax.ShapeDtypeStruct(s, F32) for s in shapes)
    scratch = [
        pltpu.VMEM((CH * BX * BZ, BY), F32),
        pltpu.VMEM((PERC, HID), F32),
        pltpu.VMEM((1, HID), F32),
        pltpu.VMEM((CH, HID), F32),
        pltpu.VMEM((1, CH), F32),
        pltpu.VMEM((CH * BX * BZ, BY), F32),
        pltpu.VMEM((CH * BX * BZ, BY), F32),
        pltpu.VMEM((2 * BX * BZ, BY), jnp.int32),
        pltpu.VMEM((PERC, HID), F32),
        pltpu.VMEM((1, HID), F32),
        pltpu.VMEM((CH, HID), F32),
        pltpu.VMEM((1, CH), F32),
        pltpu.VMEM((2, BX + 2, BZ + 2, CH, BY), F32),
        pltpu.VMEM((2, 8, 128), F32),
        pltpu.VMEM((2, 2, 3, 3, 8, 128), F32),
        pltpu.VMEM((2, BX + 2, BZ + 2, CH, BY), F32),
        pltpu.VMEM((2, 2, 2, 8, 128), F32),
        pltpu.VMEM((2, 2, BZ, CH, BY), F32),
        pltpu.VMEM((2, BX, 2, CH, BY), F32),
        pltpu.VMEM((2, 2, 2, CH, BY), F32),
        pltpu.VMEM((2, 2, 3, 3, 2, 8, 128), F32),
        pltpu.VMEM((2, BX, P_ROWS, ROW), BF16),
        pltpu.VMEM((2, BX, H_ROWS, ROW), BF16),
        pltpu.VMEM((2, BX, HID, ROW), F32),
        pltpu.VMEM((BX, 3 * HID + 3 * CH, ROW), BF16),
        pltpu.VMEM((BX, BZ, CH, BY), F32),
        pltpu.VMEM((BX + 4, 3, BZ + 2, CH, BY), F32),
        pltpu.VMEM((12, 128, 128), F32),
        pltpu.VMEM((12, 128, 128), BF16),
        pltpu.VMEM((256, 128), F32),
        pltpu.VMEM((HID, P_ROWS), BF16),
        pltpu.VMEM((CH, H_ROWS), BF16),
        pltpu.VMEM((HID, 3 * CH), BF16),
        pltpu.VMEM((PERC, 3 * HID), BF16),
        pltpu.VMEM((128, 128), F32),
        pltpu.VMEM((48, 128), F32),
        pltpu.VMEM((24, 128), F32),
        pltpu.VMEM((sizes[1] * sizes[2], 24, 128), F32),
        pltpu.VMEM((sizes[0] // 2, 24, 128), F32),
        pltpu.VMEM((48, 128), F32),
        pltpu.VMEM((BACK, 128), F32),
        pltpu.SemaphoreType.DMA((7,)),
        pltpu.SemaphoreType.DMA((5,)),
        pltpu.SemaphoreType.DMA((4,)),
        pltpu.SemaphoreType.DMA((4,)),
        pltpu.SemaphoreType.DMA((4,)),
        pltpu.SemaphoreType.DMA((4,)),
    ]
    outs = pl.pallas_call(
        functools.partial(kernel, sizes),
        out_shape=shapes,
        in_specs=[hbm] * 7,
        out_specs=(hbm,) * 5,
        scratch_shapes=scratch,
        compiler_params=pltpu.CompilerParams(
            collective_id=0, has_side_effects=True, vmem_limit_bytes=60 * 1024 * 1024),
        cost_estimate=pl.CostEstimate(flops=2 * 10**8, bytes_accessed=10**6, transcendentals=524288),
        name="automaton",
    )(
        start_state.reshape(CH * BX * BZ, BY),
        cotangent.reshape(CH * BX * BZ, BY),
        update_masks.reshape(2 * BX * BZ, BY),
        first_weight, first_bias.reshape(1, HID), second_weight.T, second_bias.reshape(1, CH),
    )
    grad, gw1, gb1, gw2, gb2 = pl.pallas_call(
        write_out,
        out_shape=shapes,
        in_specs=[pl.BlockSpec(memory_space=pltpu.VMEM)] * 5,
        out_specs=(hbm,) * 5,
        scratch_shapes=[pltpu.SemaphoreType.DMA((5,))],
        cost_estimate=pl.CostEstimate(flops=0, bytes_accessed=600000, transcendentals=0),
        name="write_out",
    )(*outs)
    return grad.reshape(CH, BX, BZ, BY), gw1, gb1.reshape(HID), gw2.T, gb2.reshape(CH)


def solution(mesh):
    grid = P(None, "gx", "gz", "gy")
    return jax.shard_map(
        body, mesh=mesh,
        in_specs=(grid, grid, grid, P(), P(), P(), P()),
        out_specs=(grid, P(), P(), P(), P()),
        check_vma=False)
```

```python
import functools
import math

import jax
import jax.numpy as jnp
from jax import lax
from jax.experimental import pallas as pl
from jax.experimental.pallas import tpu as pltpu
from jax.sharding import PartitionSpec as P

MESH = pl.DeviceIdType.MESH
F32 = jnp.float32
BF16 = jnp.bfloat16

CH, HID, PERC = 16, 64, 48
BX, BZ, BY = 4, 8, 128
ROW = BZ * BY

P_ROWS = 2 * PERC + 16 + PERC
H_ROWS = 2 * HID + 16 + HID

DIRS = [(dx, dy, dz) for dx in (-1, 0, 1) for dy in (-1, 0, 1) for dz in (-1, 0, 1) if (dx, dy, dz) != (0, 0, 0)]
DIRS = sorted(DIRS, key=lambda d: -sum(map(abs, d)))
ACROSS = [d for d in DIRS if d[0] != 0]
WITHIN = [d for d in DIRS if d[0] == 0]
SIDE_PLANES, MID_PLANES = (0, BX - 1), tuple(range(1, BX - 1))

HALO = 2 * BZ * CH + 2 * BX * CH + 4 * CH + 18 * 8


def high(value):
    return value.astype(BF16).astype(F32)


def split3(value):
    first = high(value)
    second = high(value - first)
    return first, second, value - first - second


def span(step, length, kind):
    if step == 0:
        return pl.ds(1, length)
    if kind == "own":
        return pl.ds(1 if step < 0 else length, 1)
    return pl.ds(0 if step < 0 else length + 1, 1)


def dot(a, b):
    return lax.dot_general(a, b, (((1,), (0,)), ((), ())), preferred_element_type=F32)


def dot_nt(a, b):
    return lax.dot_general(a, b, (((1,), (1,)), ((), ())), preferred_element_type=F32)


def kernel(
    sizes,
    state_in, cot_in, mask_in, w1_in, b1_in, w2_in, b2_in,
    grad_out, gw1_out, gb1_out, gw2_out, gb2_out,
    grad_ref, gw1_ref, gb1_ref, gw2_ref, gb2_ref,
    state_ref, cot_ref, mask_ref, w1_ref, b1_ref, w2_ref, b2_ref,
    field, packs, halos, outs, opacks, rx, rz, rc, rpacks,
    percs, hids, hidden, grads, carried, zf, placed, onehot,
    tall, l1, l2, l3, l4, turn, sums, rx0, rx1, rx2, whole,
    tally, load_sem, store_sem, send_sem, recv_sem, ar_send, ar_recv,
):
    nx, ny, nz = sizes
    loads = [pltpu.make_async_copy(a, b, load_sem.at[i]) for i, (a, b) in enumerate((
        (state_in, state_ref), (w1_in, w1_ref), (b1_in, b1_ref), (w2_in, w2_ref), (b2_in, b2_ref), (cot_in, cot_ref), (mask_in, mask_ref)))]
    for c in loads:
        c.start()
    gx, gy, gz = lax.axis_index("gx"), lax.axis_index("gy"), lax.axis_index("gz")

    def device(offset):
        ox, oy, oz = offset
        return (
            lax.rem(gx + (ox % nx), nx) if ox % nx else gx,
            lax.rem(gy + (oy % ny), ny) if oy % ny else gy,
            lax.rem(gz + (oz % nz), nz) if oz % nz else gz,
        )

    def far(o):
        return -sum(min(a, n - a) for a, n in zip(o, sizes))

    plane = sorted(((0, a, b) for a in range(ny) for b in range(nz) if (a, b) != (0, 0)), key=far)
    line = sorted(((a, 0, 0) for a in range(2, nx, 2)), key=far)
    core = lax.rem(gx, 2)
    partners = []
    for o in DIRS + plane + line:
        o = (o[0] % nx, o[1] % ny, o[2] % nz)
        if o not in partners:
            partners.append(o)
    partners.sort(key=far)

    barrier = pltpu.get_barrier_semaphore()
    for o in partners:
        pl.semaphore_signal(barrier, inc=1, device_id=device(o), device_id_type=MESH)

    lane = lax.broadcasted_iota(jnp.int32, (8, 128), 1)
    sub = lax.broadcasted_iota(jnp.int32, (8, 128), 0)
    lane3 = lax.broadcasted_iota(jnp.int32, (1, 1, 128), 2)
    not_first = (lane3 > 0).astype(F32)
    not_last = (lane3 < 127).astype(F32)

    def start(copies):
        for c in copies:
            c.start()

    def wait_rows(rows, sem):
        pltpu.make_async_copy(tally.at[pl.ds(0, rows)], tally.at[pl.ds(0, rows)], sem).wait()

    def pack_state(k, x):
        turned = field[k, x + 1, pl.ds(1, BZ)].reshape(128, 128).T
        for r, row in ((x, 0), (x + 4, 127)):
            packs[k, 1, r : r + 1] = turned[row : row + 1]
            if x in SIDE_PLANES:
                packs[k, 0, r : r + 1] = turned[row : row + 1]

    loads[0].wait()
    for x in range(BX):
        for z in range(BZ):
            field[0, x + 1, z + 1] = state_ref[pl.ds(x * BZ + z, CH, stride=BX * BZ), :]
    for k in range(2):
        packs[k, 0] = jnp.zeros((8, 128), F32)
        opacks[k, 0] = jnp.zeros_like(opacks[k, 0])
    for x in range(BX):
        pack_state(0, x)

    def state_copies(k, dirs):
        copies = []
        for d in dirs:
            if d[1]:
                src = packs.at[k, 0 if d[0] else 1]
                dst = halos.at[k, 0 if d[1] > 0 else 1, 1 - d[0], 1 - d[2]]
            else:
                src = field.at[k, span(d[0], BX, "own"), span(d[2], BZ, "own")]
                dst = field.at[k, span(-d[0], BX, "halo"), span(-d[2], BZ, "halo")]
            copies.append(pltpu.make_async_remote_copy(
                src_ref=src, dst_ref=dst, send_sem=send_sem.at[k], recv_sem=recv_sem.at[k],
                device_id=device(d), device_id_type=MESH))
        return copies

    def out_copies(k, dirs):
        copies = []
        for d in dirs:
            at_x, at_z = pl.ds(0 if d[0] > 0 else 1, 1), pl.ds(0 if d[2] > 0 else 1, 1)
            if d[1]:
                src = opacks.at[k, 0 if d[0] else 1, 0 if d[1] < 0 else 1, 1 if d[2] else 0]
                dst = rpacks.at[k, 0 if d[1] > 0 else 1, 1 - d[0], 1 - d[2]]
            else:
                src = outs.at[k, span(d[0], BX, "halo"), span(d[2], BZ, "halo")]
                if d[0] and d[2]:
                    dst = rc.at[k, at_x, at_z]
                elif d[0]:
                    dst = rx.at[k, at_x]
                else:
                    dst = rz.at[k, :, at_z]
            copies.append(pltpu.make_async_remote_copy(
                src_ref=src, dst_ref=dst, send_sem=send_sem.at[2 + k], recv_sem=recv_sem.at[2 + k],
                device_id=device(d), device_id_type=MESH))
        return copies

    pl.semaphore_wait(barrier, len(partners))
    start(state_copies(0, DIRS))

    for c in loads[1:5]:
        c.wait()
    tall[...] = jnp.zeros_like(tall)
    w1 = w1_ref[...] * 0.125
    w1h = high(w1)
    tall[0:48, 0:64] = w1h
    tall[48:96, 0:64] = w1h
    b1 = split3(b1_ref[...])
    for s in range(3):
        tall[96 + s : 97 + s, 0:64] = b1[s]
    tall[112:160, 0:64] = w1 - w1h
    l1[...] = tall[...].T[0:64, 0:P_ROWS].astype(BF16)

    tall[...] = jnp.zeros_like(tall)
    w2t = w2_ref[...]
    tall[0:16, 0:64] = w2t
    w2 = tall[...].T[0:64, 0:16]
    tall[...] = jnp.zeros_like(tall)
    w2h = high(w2)
    tall[0:64, 0:16] = w2h
    tall[64:128, 0:16] = w2h
    b2 = split3(b2_ref[...])
    for s in range(3):
        tall[128 + s : 129 + s, 0:16] = b2[s]
    tall[144:208, 0:16] = w2 - w2h
    l2[...] = tall[...].T[0:16, 0:H_ROWS].astype(BF16)

    tall[...] = jnp.zeros_like(tall)
    tall[0:48, 0:64] = -w1
    w1t = tall[...].T[0:64, 0:48]
    tall[...] = jnp.zeros_like(tall)
    w1th = high(w1t)
    tall[0:64, 0:48] = w1t - w1th
    tall[64:128, 0:48] = w1th
    tall[128:192, 0:48] = w1th
    l4[...] = tall[...].T[0:48, 0:192].astype(BF16)

    tall[...] = jnp.zeros_like(tall)
    w2th = high(w2t)
    tall[0:16, 0:64] = w2th
    tall[16:32, 0:64] = w2th
    tall[32:48, 0:64] = w2t - w2th
    l3[...] = tall[...].T[0:64, 0:48].astype(BF16)

    kk = lax.broadcasted_iota(jnp.int32, (128, 128), 0)
    yy = lax.broadcasted_iota(jnp.int32, (128, 128), 1)
    feature = lax.rem(lax.div(kk, 8), 3)
    row8 = lax.rem(kk, 8)
    hit = jnp.logical_and(kk < 72, yy == jnp.where(row8 < 4, 127, 0))
    for x in range(BX):
        for f in range(3):
            sign = jnp.where(row8 < 4, 1.0, -1.0) if f == 1 else 1.0
            onehot[x * 3 + f] = jnp.where(
                jnp.logical_and(hit, jnp.logical_and(feature == f, lax.rem(row8, 4) == x)), sign, 0.0
            ).astype(BF16)
    turn[...] = jnp.zeros_like(turn)
    for k in range(2):
        for x in range(BX):
            percs[k, x, 2 * PERC : 2 * PERC + 16, :] = jnp.ones((16, ROW), BF16)
            hids[k, x, 2 * HID : 2 * HID + 16, :] = jnp.ones((16, ROW), BF16)
    for x in (0, 1, BX + 2, BX + 3):
        zf[x] = jnp.zeros_like(zf[x])
    for c in loads[5:]:
        c.wait()
    for x in range(BX):
        for z in range(BZ):
            carried[x, z] = cot_ref[pl.ds(x * BZ + z, CH, stride=BX * BZ), :]

    low_x, top_x = (gx > 0).astype(F32), (gx < nx - 1).astype(F32)
    low_y, top_y = (gy > 0).astype(F32), (gy < ny - 1).astype(F32)
    low_z, top_z = (gz > 0).astype(F32), (gz < nz - 1).astype(F32)
    in_x, in_z = (low_x, 1.0, top_x), (low_z, 1.0, top_z)

    def halves(value):
        hi = value.astype(BF16)
        return hi, (value - hi.astype(F32)).astype(BF16)

    def place(rows24, features):
        parts = split3(rows24)
        n = 8 * features
        for s in range(3):
            turn[24 * s : 24 * s + n, :] = parts[s]
        turned = turn[...].T.astype(BF16)
        for x in range(BX):
            for f in range(features):
                placed[x * 3 + f] = dot(turned, onehot[x * 3 + f])

    def clear_outside(k):
        @pl.when(gx == 0)
        def _():
            field[k, 0] = jnp.zeros_like(field[k, 0])
        @pl.when(gx == nx - 1)
        def _():
            field[k, BX + 1] = jnp.zeros_like(field[k, BX + 1])
        @pl.when(gz == 0)
        def _():
            field[k, :, 0] = jnp.zeros_like(field[k, :, 0])
        @pl.when(gz == nz - 1)
        def _():
            field[k, :, BZ + 1] = jnp.zeros_like(field[k, :, BZ + 1])

    def filter_columns(k):
        grid = {}
        for ix in range(3):
            for iz in range(3):
                tile = jnp.where(sub < 4, halos[k, 1, ix, iz] * top_y, halos[k, 0, ix, iz] * low_y)
                grid[ix, iz] = tile * (in_x[ix] * in_z[iz])
        xs, xd = [], []
        for iz in range(3):
            mid = grid[1, iz]
            after = pltpu.roll(jnp.where(lax.rem(sub, 4) == 0, pltpu.roll(grid[2, iz], 4, 0), mid), 7, 0)
            before = pltpu.roll(jnp.where(lax.rem(sub, 4) == 3, pltpu.roll(grid[0, iz], 4, 0), mid), 1, 0)
            xs.append(before + 2.0 * mid + after)
            xd.append(after - before)

        def around(t):
            above = pltpu.roll(jnp.where(lane < 16, t[2], t[1]), 112, 1)
            below = pltpu.roll(jnp.where(lane >= 112, t[0], t[1]), 16, 1)
            return below, above

        d_below, d_above = around(xd)
        s_below, s_above = around(xs)
        place(jnp.concatenate([
            d_below + 2.0 * xd[1] + d_above,
            s_below + 2.0 * xs[1] + s_above,
            s_above - s_below], axis=0), 3)

    def forward(k, x):
        zs, zd = [], []
        for i in range(3):
            v = field[k, x + i]
            zs.append(v[0:8] + 2.0 * v[1:9] + v[2:10])
            zd.append(v[2:10] - v[0:8])
        b = zs[2] - zs[0]
        a = zs[0] + 2.0 * zs[1] + zs[2]
        c = zd[0] + 2.0 * zd[1] + zd[2]
        up = lambda t: pltpu.roll(t, 127, 2) * not_last
        down = lambda t: pltpu.roll(t, 1, 2) * not_first
        features = (
            2.0 * b + up(b) + down(b),
            up(a) - down(a),
            2.0 * c + up(c) + down(c),
        )
        for f in range(3):
            perc = features[f] + placed[x * 3 + f].reshape(BZ, CH, BY)
            flat = jnp.concatenate([perc[z] for z in range(BZ)], axis=1)
            hi, lo = halves(flat)
            percs[k, x, f * 16 : f * 16 + 16] = hi
            percs[k, x, 48 + f * 16 : 64 + f * 16] = lo
            percs[k, x, 112 + f * 16 : 128 + f * 16] = hi
        hid = jnp.tanh(dot(l1[...], percs[k, x]))
        hidden[k, x] = hid
        hi, lo = halves(hid)
        hids[k, x, 0:64] = hi
        hids[k, x, 64:128] = lo
        hids[k, x, 144:208] = hi

    def advance(x):
        update = dot(l2[...], hids[0, x])
        mask = mask_ref[x * BZ : (x + 1) * BZ, :].astype(F32)
        for z in range(BZ):
            field[1, x + 1, z + 1] = field[0, x + 1, z + 1] + mask[z : z + 1] * update[:, z * BY : (z + 1) * BY]
        pack_state(1, x)

    def cells(k, x):
        mask = mask_ref[(k * BX + x) * BZ : (k * BX + x + 1) * BZ, :].astype(F32)
        g = carried[x]
        du = jnp.concatenate([mask[z : z + 1] * g[z] for z in range(BZ)], axis=1)
        hi, lo = halves(du)
        grads[x, 192:208] = hi
        grads[x, 208:224] = lo
        grads[x, 224:240] = hi
        hid = hidden[k, x]
        dz = dot(l3[...], grads[x, 192:240]) * (1.0 - hid * hid)
        hi, lo = halves(dz)
        grads[x, 0:64] = hi
        grads[x, 64:128] = hi
        grads[x, 128:192] = lo

    def spread(x):
        dp = dot(l4[...], grads[x, 0:192])
        zero = jnp.zeros((2, CH, BY), F32)
        for f in range(3):
            q = jnp.concatenate(
                [zero] + [dp[f * 16 : f * 16 + 16, z * BY : (z + 1) * BY].reshape(1, CH, BY) for z in range(BZ)] + [zero], axis=0)
            zf[x + 2, f] = q[2:12] - q[0:10] if f == 2 else q[0:10] + 2.0 * q[1:11] + q[2:12]

    def gather(k, xo):
        pr = zf[xo + 2, 0] - zf[xo, 0] + zf[xo, 2] + 2.0 * zf[xo + 1, 2] + zf[xo + 2, 2]
        q = zf[xo, 1] + 2.0 * zf[xo + 1, 1] + zf[xo + 2, 1]
        up, down = pr + q, pr - q
        outs[k, xo] = 2.0 * pr + pltpu.roll(down, 1, 2) * not_first + pltpu.roll(up, 127, 2) * not_last
        both = jnp.where(lane3 == 0, up, down)
        main = both[1:9].reshape(128, 128).T
        side = jnp.concatenate([both[0], both[9]], axis=0)
        side = jnp.concatenate([side, jnp.zeros((96, 128), F32)], axis=0).T
        tile = 0 if xo in (0, BX + 1) else 1
        for s, r in ((0, 0), (1, 127)):
            opacks[k, tile, s, 0, xo : xo + 1] = main[r : r + 1]
            opacks[k, tile, s, 1, xo : xo + 1] = side[r : r + 1]

    def add_halo(k):
        total = jnp.zeros((8, 128), F32)
        for iy in range(2):
            base = 4 if iy == 0 else 0
            in_y = low_y if iy == 0 else top_y
            for ix in range(3):
                part = jnp.zeros((8, 128), F32)
                for iz in range(3):
                    if iz == 1:
                        t = rpacks[k, iy, ix, iz]
                    else:
                        t = pltpu.roll(rpacks[k, iy, ix, iz], 112, 1)
                        t = jnp.where(lane < 16 if iz == 0 else lane >= 112, t, 0.0)
                    part = part + t * (in_y * in_x[ix] * in_z[iz])
                if ix == 1:
                    part = jnp.where(lax.div(sub, 4) == base // 4, pltpu.roll(part, 3 if iy == 0 else 7, 0), 0.0)
                else:
                    row = base if ix == 0 else base + 3
                    part = jnp.where(sub == row, pltpu.roll(part, 7 if iy == 0 else 3, 0), 0.0)
                total = total + part
        place(total, 1)

        def body(x, _):
            carried[x] = carried[x] + outs[k, x + 1, pl.ds(1, BZ)] + placed[x * 3].reshape(BZ, CH, BY)
            return 0
        lax.fori_loop(0, BX, body, 0, unroll=True)
        for ix in range(2):
            x = 0 if ix == 0 else BX - 1
            m = low_x if ix == 0 else top_x
            carried[x] = carried[x] + rx[k, ix] * m
            for iz in range(2):
                z = 0 if iz == 0 else BZ - 1
                carried[x, z] = carried[x, z] + rc[k, ix, iz] * (m * (low_z if iz == 0 else top_z))
        for iz in range(2):
            z = 0 if iz == 0 else BZ - 1
            m = low_z if iz == 0 else top_z
            carried[:, z] = carried[:, z] + rz[k, :, iz] * m

    def weight_grads(k):
        def body(x, acc):
            g1, g2 = acc
            g1 = g1 + dot_nt(percs[k, x, 0:112], grads[x, 64:224])
            g2 = g2 + dot_nt(grads[x, 192:224], hids[k, x, 0:128])
            return g1, g2
        return lax.fori_loop(0, BX, body, (jnp.zeros((112, 160), F32), jnp.zeros((32, 128), F32)), unroll=True)

    wait_rows(HALO, recv_sem.at[0])
    clear_outside(0)
    filter_columns(0)
    for x in SIDE_PLANES:
        forward(0, x)
        advance(x)
    start(state_copies(1, ACROSS))
    for x in MID_PLANES:
        forward(0, x)
        advance(x)
    start(state_copies(1, WITHIN))
    wait_rows(HALO, send_sem.at[0])
    wait_rows(HALO, recv_sem.at[1])
    clear_outside(1)
    filter_columns(1)
    for x in SIDE_PLANES:
        forward(1, x)
        cells(1, x)
    for x in SIDE_PLANES:
        spread(x)
    gather(1, 0)
    gather(1, BX + 1)
    start(out_copies(1, ACROSS))
    for x in MID_PLANES:
        forward(1, x)
        cells(1, x)
        spread(x)
    for x in range(BX):
        gather(1, x + 1)
    start(out_copies(1, WITHIN))
    ga1, ga2 = weight_grads(1)
    wait_rows(HALO, send_sem.at[1])
    wait_rows(HALO, recv_sem.at[3])
    add_halo(1)
    for x in range(BX):
        cells(0, x)
    gb1, gb2 = weight_grads(0)
    g1, g2 = ga1 + gb1, ga2 + gb2

    both = (g1[0:48] + g1[48:96])[:, 0:128]
    both = (both + pltpu.roll(both, 64, 1)) * 0.125
    bias1 = g1[96:104, 0:128]
    bias1 = bias1 + pltpu.roll(bias1, 64, 1)
    bias2 = jnp.concatenate([g1[96:104, 128:160], jnp.zeros((8, 96), F32)], axis=1)
    bias2 = pltpu.roll(bias2, 64, 1) + pltpu.roll(bias2, 48, 1)
    second_w = g2[0:16] + g2[16:32]
    second_w = second_w + pltpu.roll(second_w, 64, 1)
    left = lax.broadcasted_iota(jnp.int32, (16, 128), 1) < 64
    sums[0:16] = jnp.where(left, both[0:16], second_w)
    sums[16:24] = jnp.where(left[0:8], both[16:24], bias1)
    sums[24:32] = jnp.where(left[0:8], both[24:32], bias2)
    sums[32:48] = both[32:48]

    half = sums.shape[0] // 2
    own_rows = pl.ds(pl.multiple_of(core * half, 8), half)
    other_rows = pl.ds(pl.multiple_of((1 - core) * half, 8), half)
    twin = (gx + 1 - 2 * core, gy, gz)
    mine = gy * nz + gz
    chip = lax.div(gx, 2)
    pair = pltpu.make_async_remote_copy(
        src_ref=sums.at[other_rows], dst_ref=rx0, send_sem=ar_send.at[0], recv_sem=ar_recv.at[0],
        device_id=twin, device_id_type=MESH)
    pair.start()
    pair.wait_recv()
    rx1[mine] = sums[own_rows] + rx0[...]
    stage1 = [pltpu.make_async_remote_copy(
        src_ref=rx1.at[mine], dst_ref=rx1.at[mine], send_sem=ar_send.at[1], recv_sem=ar_recv.at[1],
        device_id=device(o), device_id_type=MESH) for o in plane]
    start(stage1)
    pair.wait_send()
    for x in SIDE_PLANES:
        spread(x)
    gather(0, 0)
    gather(0, BX + 1)
    start(out_copies(0, ACROSS))
    for x in MID_PLANES:
        spread(x)
    for x in range(BX):
        gather(0, x + 1)
    start(out_copies(0, WITHIN))
    wait_rows(half * len(plane), ar_recv.at[1])
    wait_rows(half * len(plane), ar_send.at[1])
    total = rx1[0]
    for i in range(1, ny * nz):
        total = total + rx1[i]
    rx2[chip] = total
    stage2 = [pltpu.make_async_remote_copy(
        src_ref=rx2.at[chip], dst_ref=rx2.at[chip], send_sem=ar_send.at[2], recv_sem=ar_recv.at[2],
        device_id=device(o), device_id_type=MESH) for o in line]
    start(stage2)
    wait_rows(HALO, send_sem.at[3])
    wait_rows(HALO, recv_sem.at[2])
    add_halo(0)
    for x in range(BX):
        for z in range(BZ):
            grad_ref[pl.ds(x * BZ + z, CH, stride=BX * BZ), :] = carried[x, z]
    stores = [pltpu.make_async_copy(a, b, store_sem.at[i]) for i, (a, b) in enumerate((
        (grad_ref, grad_out), (gw1_ref, gw1_out), (gb1_ref, gb1_out), (gw2_ref, gw2_out), (gb2_ref, gb2_out)))]
    stores[0].start()
    wait_rows(HALO, send_sem.at[2])
    wait_rows(half * len(line), ar_recv.at[2])
    wait_rows(half * len(line), ar_send.at[2])
    total = rx2[0]
    for i in range(1, nx // 2):
        total = total + rx2[i]
    whole[own_rows] = total
    share = pltpu.make_async_remote_copy(
        src_ref=whole.at[own_rows], dst_ref=whole.at[own_rows], send_sem=ar_send.at[3], recv_sem=ar_recv.at[3],
        device_id=twin, device_id_type=MESH)
    share.start()
    share.wait()
    scale = 1.0 / math.sqrt(nx * BX * ny * BY * nz * BZ)
    final = whole[...] * scale
    gw1_ref[...] = final[:, 0:64]
    gb1_ref[...] = final[16:17, 64:128]
    gw2_ref[...] = final[0:16, 64:128]
    gb2_ref[...] = final[24:25, 64:80]
    for c in stores[1:]:
        c.start()
    for c in stores:
        c.wait()


def write_out(*refs):
    sems = refs[-1]
    copies = [pltpu.make_async_copy(refs[i], refs[5 + i], sems.at[i]) for i in range(5)]
    for c in copies:
        c.start()
    for c in copies:
        c.wait()


def body(start_state, cotangent, update_masks, first_weight, first_bias, second_weight, second_bias):
    sizes = (lax.axis_size("gx"), lax.axis_size("gy"), lax.axis_size("gz"))
    hbm = pl.BlockSpec(memory_space=pltpu.HBM)
    shapes = ((CH * BX * BZ, BY), (PERC, HID), (1, HID), (CH, HID), (1, CH))
    shapes = tuple(jax.ShapeDtypeStruct(s, F32) for s in shapes)
    scratch = [
        pltpu.VMEM((CH * BX * BZ, BY), F32),
        pltpu.VMEM((PERC, HID), F32),
        pltpu.VMEM((1, HID), F32),
        pltpu.VMEM((CH, HID), F32),
        pltpu.VMEM((1, CH), F32),
        pltpu.VMEM((CH * BX * BZ, BY), F32),
        pltpu.VMEM((CH * BX * BZ, BY), F32),
        pltpu.VMEM((2 * BX * BZ, BY), jnp.int32),
        pltpu.VMEM((PERC, HID), F32),
        pltpu.VMEM((1, HID), F32),
        pltpu.VMEM((CH, HID), F32),
        pltpu.VMEM((1, CH), F32),
        pltpu.VMEM((2, BX + 2, BZ + 2, CH, BY), F32),
        pltpu.VMEM((2, 2, 8, 128), F32),
        pltpu.VMEM((2, 2, 3, 3, 8, 128), F32),
        pltpu.VMEM((2, BX + 2, BZ + 2, CH, BY), F32),
        pltpu.VMEM((2, 2, 2, 2, 8, 128), F32),
        pltpu.VMEM((2, 2, BZ, CH, BY), F32),
        pltpu.VMEM((2, BX, 2, CH, BY), F32),
        pltpu.VMEM((2, 2, 2, CH, BY), F32),
        pltpu.VMEM((2, 2, 3, 3, 8, 128), F32),
        pltpu.VMEM((2, BX, P_ROWS, ROW), BF16),
        pltpu.VMEM((2, BX, H_ROWS, ROW), BF16),
        pltpu.VMEM((2, BX, HID, ROW), F32),
        pltpu.VMEM((BX, 3 * HID + 3 * CH, ROW), BF16),
        pltpu.VMEM((BX, BZ, CH, BY), F32),
        pltpu.VMEM((BX + 4, 3, BZ + 2, CH, BY), F32),
        pltpu.VMEM((12, 128, 128), F32),
        pltpu.VMEM((12, 128, 128), BF16),
        pltpu.VMEM((256, 128), F32),
        pltpu.VMEM((HID, P_ROWS), BF16),
        pltpu.VMEM((CH, H_ROWS), BF16),
        pltpu.VMEM((HID, 3 * CH), BF16),
        pltpu.VMEM((PERC, 3 * HID), BF16),
        pltpu.VMEM((128, 128), F32),
        pltpu.VMEM((48, 128), F32),
        pltpu.VMEM((24, 128), F32),
        pltpu.VMEM((sizes[1] * sizes[2], 24, 128), F32),
        pltpu.VMEM((sizes[0] // 2, 24, 128), F32),
        pltpu.VMEM((48, 128), F32),
        pltpu.VMEM((HALO, 128), F32),
        pltpu.SemaphoreType.DMA((7,)),
        pltpu.SemaphoreType.DMA((5,)),
        pltpu.SemaphoreType.DMA((4,)),
        pltpu.SemaphoreType.DMA((4,)),
        pltpu.SemaphoreType.DMA((4,)),
        pltpu.SemaphoreType.DMA((4,)),
    ]
    outs = pl.pallas_call(
        functools.partial(kernel, sizes),
        out_shape=shapes,
        in_specs=[hbm] * 7,
        out_specs=(hbm,) * 5,
        scratch_shapes=scratch,
        compiler_params=pltpu.CompilerParams(
            collective_id=0, has_side_effects=True, vmem_limit_bytes=60 * 1024 * 1024),
        cost_estimate=pl.CostEstimate(flops=2 * 10**8, bytes_accessed=10**6, transcendentals=524288),
        name="automaton",
    )(
        start_state.reshape(CH * BX * BZ, BY),
        cotangent.reshape(CH * BX * BZ, BY),
        update_masks.reshape(2 * BX * BZ, BY),
        first_weight, first_bias.reshape(1, HID), second_weight.T, second_bias.reshape(1, CH),
    )
    grad, gw1, gb1, gw2, gb2 = pl.pallas_call(
        write_out,
        out_shape=shapes,
        in_specs=[pl.BlockSpec(memory_space=pltpu.VMEM)] * 5,
        out_specs=(hbm,) * 5,
        scratch_shapes=[pltpu.SemaphoreType.DMA((5,))],
        cost_estimate=pl.CostEstimate(flops=0, bytes_accessed=600000, transcendentals=0),
        name="write_out",
    )(*outs)
    return grad.reshape(CH, BX, BZ, BY), gw1, gb1.reshape(HID), gw2.T, gb2.reshape(CH)


def solution(mesh):
    grid = P(None, "gx", "gz", "gy")
    return jax.shard_map(
        body, mesh=mesh,
        in_specs=(grid, grid, grid, P(), P(), P(), P()),
        out_specs=(grid, P(), P(), P(), P()),
        check_vma=False)
```

```python
import functools
import math

import jax
import jax.numpy as jnp
from jax import lax
from jax.experimental import pallas as pl
from jax.experimental.pallas import tpu as pltpu
from jax.sharding import PartitionSpec as P

MESH = pl.DeviceIdType.MESH
F32 = jnp.float32
BF16 = jnp.bfloat16

CH, HID, PERC = 16, 64, 48
BX, BZ, BY = 4, 8, 128
ROW = BZ * BY

P_ROWS = 2 * PERC + 16 + PERC
H_ROWS = 2 * HID + 16 + HID

DIRS = [(dx, dy, dz) for dx in (-1, 0, 1) for dy in (-1, 0, 1) for dz in (-1, 0, 1) if (dx, dy, dz) != (0, 0, 0)]
DIRS = sorted(DIRS, key=lambda d: -sum(map(abs, d)))
ACROSS = [d for d in DIRS if d[0] != 0]
WITHIN = [d for d in DIRS if d[0] == 0]
SIDE_PLANES, MID_PLANES = (0, BX - 1), tuple(range(1, BX - 1))

HALO = 2 * BZ * CH + 2 * BX * CH + 4 * CH + 18 * 8


def high(value):
    return value.astype(BF16).astype(F32)


def split3(value):
    first = high(value)
    second = high(value - first)
    return first, second, value - first - second


def span(step, length, kind):
    if step == 0:
        return pl.ds(1, length)
    if kind == "own":
        return pl.ds(1 if step < 0 else length, 1)
    return pl.ds(0 if step < 0 else length + 1, 1)


def dot(a, b):
    return lax.dot_general(a, b, (((1,), (0,)), ((), ())), preferred_element_type=F32)


def dot_nt(a, b):
    return lax.dot_general(a, b, (((1,), (1,)), ((), ())), preferred_element_type=F32)


def kernel(
    sizes,
    state_in, cot_in, mask_in, w1_in, b1_in, w2_in, b2_in,
    grad_out, sums_out,
    grad_ref,
    state_ref, cot_ref, mask_ref, w1_ref, b1_ref, w2_ref, b2_ref,
    field, packs, halos, outs, opacks, rx, rz, rc, rpacks,
    percs, hids, hidden, grads, carried, zf, placed, onehot,
    tall, l1, l2, l3, l4, turn, sums, rx0, rx1, rx2, whole, zline,
    tally, load_sem, store_sem, send_sem, recv_sem, ar_send, ar_recv,
):
    nx, ny, nz = sizes
    loads = [pltpu.make_async_copy(a, b, load_sem.at[i]) for i, (a, b) in enumerate((
        (state_in, state_ref), (w1_in, w1_ref), (b1_in, b1_ref), (w2_in, w2_ref), (b2_in, b2_ref), (cot_in, cot_ref), (mask_in, mask_ref)))]
    for c in loads:
        c.start()
    gx, gy, gz = lax.axis_index("gx"), lax.axis_index("gy"), lax.axis_index("gz")

    def device(offset):
        ox, oy, oz = offset
        return (
            lax.rem(gx + (ox % nx), nx) if ox % nx else gx,
            lax.rem(gy + (oy % ny), ny) if oy % ny else gy,
            lax.rem(gz + (oz % nz), nz) if oz % nz else gz,
        )

    def far(o):
        return -sum(min(a, n - a) for a, n in zip(o, sizes))

    plane = sorted(((0, a, b) for a in range(ny) for b in range(nz) if (a, b) != (0, 0)), key=far)
    line = sorted(((a, 0, 0) for a in range(2, nx, 2)), key=far)
    core = lax.rem(gx, 2)
    partners = []
    for o in DIRS + plane + line:
        o = (o[0] % nx, o[1] % ny, o[2] % nz)
        if o not in partners:
            partners.append(o)
    partners.sort(key=far)

    barrier = pltpu.get_barrier_semaphore()
    for o in partners:
        pl.semaphore_signal(barrier, inc=1, device_id=device(o), device_id_type=MESH)

    lane = lax.broadcasted_iota(jnp.int32, (8, 128), 1)
    sub = lax.broadcasted_iota(jnp.int32, (8, 128), 0)
    lane3 = lax.broadcasted_iota(jnp.int32, (1, 1, 128), 2)
    not_first = (lane3 > 0).astype(F32)
    not_last = (lane3 < 127).astype(F32)

    def start(copies):
        for c in copies:
            c.start()

    def wait_rows(rows, sem):
        pltpu.make_async_copy(tally.at[pl.ds(0, rows)], tally.at[pl.ds(0, rows)], sem).wait()

    def pack_state(k, x):
        turned = field[k, x + 1, pl.ds(1, BZ)].reshape(128, 128).T
        for r, row in ((x, 0), (x + 4, 127)):
            packs[k, 1, r : r + 1] = turned[row : row + 1]
            if x in SIDE_PLANES:
                packs[k, 0, r : r + 1] = turned[row : row + 1]

    loads[0].wait()
    for x in range(BX):
        for z in range(BZ):
            field[0, x + 1, z + 1] = state_ref[pl.ds(x * BZ + z, CH, stride=BX * BZ), :]
    for k in range(2):
        packs[k, 0] = jnp.zeros((8, 128), F32)
        opacks[k, 0] = jnp.zeros_like(opacks[k, 0])
    for x in range(BX):
        pack_state(0, x)

    def state_copies(k, dirs):
        copies = []
        for d in dirs:
            if d[1]:
                src = packs.at[k, 0 if d[0] else 1]
                dst = halos.at[k, 0 if d[1] > 0 else 1, 1 - d[0], 1 - d[2]]
            else:
                src = field.at[k, span(d[0], BX, "own"), span(d[2], BZ, "own")]
                dst = field.at[k, span(-d[0], BX, "halo"), span(-d[2], BZ, "halo")]
            copies.append(pltpu.make_async_remote_copy(
                src_ref=src, dst_ref=dst, send_sem=send_sem.at[k], recv_sem=recv_sem.at[k],
                device_id=device(d), device_id_type=MESH))
        return copies

    def out_copies(k, dirs):
        copies = []
        for d in dirs:
            at_x, at_z = pl.ds(0 if d[0] > 0 else 1, 1), pl.ds(0 if d[2] > 0 else 1, 1)
            if d[1]:
                src = opacks.at[k, 0 if d[0] else 1, 0 if d[1] < 0 else 1, 1 if d[2] else 0]
                dst = rpacks.at[k, 0 if d[1] > 0 else 1, 1 - d[0], 1 - d[2]]
            else:
                src = outs.at[k, span(d[0], BX, "halo"), span(d[2], BZ, "halo")]
                if d[0] and d[2]:
                    dst = rc.at[k, at_x, at_z]
                elif d[0]:
                    dst = rx.at[k, at_x]
                else:
                    dst = rz.at[k, :, at_z]
            copies.append(pltpu.make_async_remote_copy(
                src_ref=src, dst_ref=dst, send_sem=send_sem.at[2 + k], recv_sem=recv_sem.at[2 + k],
                device_id=device(d), device_id_type=MESH))
        return copies

    pl.semaphore_wait(barrier, len(partners))
    start(state_copies(0, DIRS))

    for c in loads[1:5]:
        c.wait()
    tall[...] = jnp.zeros_like(tall)
    w1 = w1_ref[...] * 0.125
    w1h = high(w1)
    tall[0:48, 0:64] = w1h
    tall[48:96, 0:64] = w1h
    b1 = split3(b1_ref[...])
    for s in range(3):
        tall[96 + s : 97 + s, 0:64] = b1[s]
    tall[112:160, 0:64] = w1 - w1h
    l1[...] = tall[...].T[0:64, 0:P_ROWS].astype(BF16)

    tall[...] = jnp.zeros_like(tall)
    w2t = w2_ref[...]
    tall[0:16, 0:64] = w2t
    w2 = tall[...].T[0:64, 0:16]
    tall[...] = jnp.zeros_like(tall)
    w2h = high(w2)
    tall[0:64, 0:16] = w2h
    tall[64:128, 0:16] = w2h
    b2 = split3(b2_ref[...])
    for s in range(3):
        tall[128 + s : 129 + s, 0:16] = b2[s]
    tall[144:208, 0:16] = w2 - w2h
    l2[...] = tall[...].T[0:16, 0:H_ROWS].astype(BF16)

    tall[...] = jnp.zeros_like(tall)
    tall[0:48, 0:64] = -w1
    w1t = tall[...].T[0:64, 0:48]
    tall[...] = jnp.zeros_like(tall)
    w1th = high(w1t)
    tall[0:64, 0:48] = w1t - w1th
    tall[64:128, 0:48] = w1th
    tall[128:192, 0:48] = w1th
    l4[...] = tall[...].T[0:48, 0:192].astype(BF16)

    tall[...] = jnp.zeros_like(tall)
    w2th = high(w2t)
    tall[0:16, 0:64] = w2th
    tall[16:32, 0:64] = w2th
    tall[32:48, 0:64] = w2t - w2th
    l3[...] = tall[...].T[0:64, 0:48].astype(BF16)

    kk = lax.broadcasted_iota(jnp.int32, (128, 128), 0)
    yy = lax.broadcasted_iota(jnp.int32, (128, 128), 1)
    feature = lax.rem(lax.div(kk, 8), 3)
    row8 = lax.rem(kk, 8)
    hit = jnp.logical_and(kk < 72, yy == jnp.where(row8 < 4, 127, 0))
    for x in range(BX):
        for f in range(3):
            sign = jnp.where(row8 < 4, 1.0, -1.0) if f == 1 else 1.0
            onehot[x * 3 + f] = jnp.where(
                jnp.logical_and(hit, jnp.logical_and(feature == f, lax.rem(row8, 4) == x)), sign, 0.0
            ).astype(BF16)
    turn[...] = jnp.zeros_like(turn)
    for k in range(2):
        for x in range(BX):
            percs[k, x, 2 * PERC : 2 * PERC + 16, :] = jnp.ones((16, ROW), BF16)
            hids[k, x, 2 * HID : 2 * HID + 16, :] = jnp.ones((16, ROW), BF16)
    for x in (0, 1, BX + 2, BX + 3):
        zf[x] = jnp.zeros_like(zf[x])
    for c in loads[5:]:
        c.wait()
    for x in range(BX):
        for z in range(BZ):
            carried[x, z] = cot_ref[pl.ds(x * BZ + z, CH, stride=BX * BZ), :]

    low_x, top_x = (gx > 0).astype(F32), (gx < nx - 1).astype(F32)
    low_y, top_y = (gy > 0).astype(F32), (gy < ny - 1).astype(F32)
    low_z, top_z = (gz > 0).astype(F32), (gz < nz - 1).astype(F32)
    in_x, in_z = (low_x, 1.0, top_x), (low_z, 1.0, top_z)

    def halves(value):
        hi = value.astype(BF16)
        return hi, (value - hi.astype(F32)).astype(BF16)

    def place(rows24, features):
        parts = split3(rows24)
        n = 8 * features
        for s in range(3):
            turn[24 * s : 24 * s + n, :] = parts[s]
        turned = turn[...].T.astype(BF16)
        for x in range(BX):
            for f in range(features):
                placed[x * 3 + f] = dot(turned, onehot[x * 3 + f])

    def clear_outside(k):
        @pl.when(gx == 0)
        def _():
            field[k, 0] = jnp.zeros_like(field[k, 0])
        @pl.when(gx == nx - 1)
        def _():
            field[k, BX + 1] = jnp.zeros_like(field[k, BX + 1])
        @pl.when(gz == 0)
        def _():
            field[k, :, 0] = jnp.zeros_like(field[k, :, 0])
        @pl.when(gz == nz - 1)
        def _():
            field[k, :, BZ + 1] = jnp.zeros_like(field[k, :, BZ + 1])

    def filter_columns(k):
        grid = {}
        for ix in range(3):
            for iz in range(3):
                tile = jnp.where(sub < 4, halos[k, 1, ix, iz] * top_y, halos[k, 0, ix, iz] * low_y)
                grid[ix, iz] = tile * (in_x[ix] * in_z[iz])
        xs, xd = [], []
        for iz in range(3):
            mid = grid[1, iz]
            after = pltpu.roll(jnp.where(lax.rem(sub, 4) == 0, pltpu.roll(grid[2, iz], 4, 0), mid), 7, 0)
            before = pltpu.roll(jnp.where(lax.rem(sub, 4) == 3, pltpu.roll(grid[0, iz], 4, 0), mid), 1, 0)
            xs.append(before + 2.0 * mid + after)
            xd.append(after - before)

        def around(t):
            above = pltpu.roll(jnp.where(lane < 16, t[2], t[1]), 112, 1)
            below = pltpu.roll(jnp.where(lane >= 112, t[0], t[1]), 16, 1)
            return below, above

        d_below, d_above = around(xd)
        s_below, s_above = around(xs)
        place(jnp.concatenate([
            d_below + 2.0 * xd[1] + d_above,
            s_below + 2.0 * xs[1] + s_above,
            s_above - s_below], axis=0), 3)

    ready = set()

    def forward(k, x):
        zs, zd = [], []
        for i in range(x, x + 3):
            if (k, i) not in ready:
                ready.add((k, i))
                v = field[k, i]
                zs.append(v[0:8] + 2.0 * v[1:9] + v[2:10])
                zd.append(v[2:10] - v[0:8])
                zline[i, 0], zline[i, 1] = zs[-1], zd[-1]
            else:
                zs.append(zline[i, 0])
                zd.append(zline[i, 1])
        b = zs[2] - zs[0]
        a = zs[0] + 2.0 * zs[1] + zs[2]
        c = zd[0] + 2.0 * zd[1] + zd[2]
        up = lambda t: pltpu.roll(t, 127, 2) * not_last
        down = lambda t: pltpu.roll(t, 1, 2) * not_first
        features = (
            2.0 * b + up(b) + down(b),
            up(a) - down(a),
            2.0 * c + up(c) + down(c),
        )
        for f in range(3):
            perc = features[f] + placed[x * 3 + f].reshape(BZ, CH, BY)
            flat = jnp.concatenate([perc[z] for z in range(BZ)], axis=1)
            hi, lo = halves(flat)
            percs[k, x, f * 16 : f * 16 + 16] = hi
            percs[k, x, 48 + f * 16 : 64 + f * 16] = lo
            percs[k, x, 112 + f * 16 : 128 + f * 16] = hi
        hid = jnp.tanh(dot(l1[...], percs[k, x]))
        hidden[k, x] = hid
        hi, lo = halves(hid)
        hids[k, x, 0:64] = hi
        hids[k, x, 64:128] = lo
        hids[k, x, 144:208] = hi

    def advance(x):
        update = dot(l2[...], hids[0, x])
        mask = mask_ref[x * BZ : (x + 1) * BZ, :].astype(F32)
        for z in range(BZ):
            field[1, x + 1, z + 1] = field[0, x + 1, z + 1] + mask[z : z + 1] * update[:, z * BY : (z + 1) * BY]
        pack_state(1, x)

    def cells(k, x):
        mask = mask_ref[(k * BX + x) * BZ : (k * BX + x + 1) * BZ, :].astype(F32)
        g = carried[x]
        du = jnp.concatenate([mask[z : z + 1] * g[z] for z in range(BZ)], axis=1)
        hi, lo = halves(du)
        grads[x, 192:208] = hi
        grads[x, 208:224] = lo
        grads[x, 224:240] = hi
        hid = hidden[k, x]
        dz = dot(l3[...], grads[x, 192:240]) * (1.0 - hid * hid)
        hi, lo = halves(dz)
        grads[x, 0:64] = hi
        grads[x, 64:128] = hi
        grads[x, 128:192] = lo

    def spread(x):
        dp = dot(l4[...], grads[x, 0:192])
        zero = jnp.zeros((2, CH, BY), F32)
        for f in range(3):
            q = jnp.concatenate(
                [zero] + [dp[f * 16 : f * 16 + 16, z * BY : (z + 1) * BY].reshape(1, CH, BY) for z in range(BZ)] + [zero], axis=0)
            zf[x + 2, f] = q[2:12] - q[0:10] if f == 2 else q[0:10] + 2.0 * q[1:11] + q[2:12]

    def gather(k, xo):
        pr = zf[xo + 2, 0] - zf[xo, 0] + zf[xo, 2] + 2.0 * zf[xo + 1, 2] + zf[xo + 2, 2]
        q = zf[xo, 1] + 2.0 * zf[xo + 1, 1] + zf[xo + 2, 1]
        up, down = pr + q, pr - q
        outs[k, xo] = 2.0 * pr + pltpu.roll(down, 1, 2) * not_first + pltpu.roll(up, 127, 2) * not_last
        both = jnp.where(lane3 == 0, up, down)
        main = both[1:9].reshape(128, 128).T
        side = jnp.concatenate([both[0], both[9]], axis=0)
        side = jnp.concatenate([side, jnp.zeros((96, 128), F32)], axis=0).T
        tile = 0 if xo in (0, BX + 1) else 1
        for s, r in ((0, 0), (1, 127)):
            opacks[k, tile, s, 0, xo : xo + 1] = main[r : r + 1]
            opacks[k, tile, s, 1, xo : xo + 1] = side[r : r + 1]

    def add_halo(k):
        total = jnp.zeros((8, 128), F32)
        for iy in range(2):
            base = 4 if iy == 0 else 0
            in_y = low_y if iy == 0 else top_y
            for ix in range(3):
                part = jnp.zeros((8, 128), F32)
                for iz in range(3):
                    if iz == 1:
                        t = rpacks[k, iy, ix, iz]
                    else:
                        t = pltpu.roll(rpacks[k, iy, ix, iz], 112, 1)
                        t = jnp.where(lane < 16 if iz == 0 else lane >= 112, t, 0.0)
                    part = part + t * (in_y * in_x[ix] * in_z[iz])
                if ix == 1:
                    part = jnp.where(lax.div(sub, 4) == base // 4, pltpu.roll(part, 3 if iy == 0 else 7, 0), 0.0)
                else:
                    row = base if ix == 0 else base + 3
                    part = jnp.where(sub == row, pltpu.roll(part, 7 if iy == 0 else 3, 0), 0.0)
                total = total + part
        place(total, 1)

        def body(x, _):
            carried[x] = carried[x] + outs[k, x + 1, pl.ds(1, BZ)] + placed[x * 3].reshape(BZ, CH, BY)
            return 0
        lax.fori_loop(0, BX, body, 0, unroll=True)
        for ix in range(2):
            x = 0 if ix == 0 else BX - 1
            m = low_x if ix == 0 else top_x
            carried[x] = carried[x] + rx[k, ix] * m
            for iz in range(2):
                z = 0 if iz == 0 else BZ - 1
                carried[x, z] = carried[x, z] + rc[k, ix, iz] * (m * (low_z if iz == 0 else top_z))
        for iz in range(2):
            z = 0 if iz == 0 else BZ - 1
            m = low_z if iz == 0 else top_z
            carried[:, z] = carried[:, z] + rz[k, :, iz] * m

    def weight_grads(k):
        def body(x, acc):
            g1, g2 = acc
            g1 = g1 + dot_nt(percs[k, x, 0:112], grads[x, 64:224])
            g2 = g2 + dot_nt(grads[x, 192:224], hids[k, x, 0:128])
            return g1, g2
        return lax.fori_loop(0, BX, body, (jnp.zeros((112, 160), F32), jnp.zeros((32, 128), F32)), unroll=True)

    wait_rows(HALO, recv_sem.at[0])
    clear_outside(0)
    filter_columns(0)
    for x in SIDE_PLANES:
        forward(0, x)
        advance(x)
    start(state_copies(1, ACROSS))
    for x in MID_PLANES:
        forward(0, x)
        advance(x)
    start(state_copies(1, WITHIN))
    wait_rows(HALO, send_sem.at[0])
    wait_rows(HALO, recv_sem.at[1])
    clear_outside(1)
    filter_columns(1)
    for x in SIDE_PLANES:
        forward(1, x)
        cells(1, x)
    for x in SIDE_PLANES:
        spread(x)
    gather(1, 0)
    gather(1, BX + 1)
    start(out_copies(1, ACROSS))
    for x in MID_PLANES:
        forward(1, x)
        cells(1, x)
        spread(x)
    for x in range(BX):
        gather(1, x + 1)
    start(out_copies(1, WITHIN))
    ga1, ga2 = weight_grads(1)
    wait_rows(HALO, send_sem.at[1])
    wait_rows(HALO, recv_sem.at[3])
    add_halo(1)
    for x in range(BX):
        cells(0, x)
    gb1, gb2 = weight_grads(0)
    g1, g2 = ga1 + gb1, ga2 + gb2

    both = (g1[0:48] + g1[48:96])[:, 0:128]
    both = (both + pltpu.roll(both, 64, 1)) * 0.125
    bias1 = g1[96:104, 0:128]
    bias1 = bias1 + pltpu.roll(bias1, 64, 1)
    bias2 = jnp.concatenate([g1[96:104, 128:160], jnp.zeros((8, 96), F32)], axis=1)
    bias2 = pltpu.roll(bias2, 64, 1) + pltpu.roll(bias2, 48, 1)
    second_w = g2[0:16] + g2[16:32]
    second_w = second_w + pltpu.roll(second_w, 64, 1)
    left = lax.broadcasted_iota(jnp.int32, (16, 128), 1) < 64
    sums[0:16] = jnp.where(left, both[0:16], second_w)
    sums[16:24] = jnp.where(left[0:8], both[16:24], bias1)
    sums[24:32] = jnp.where(left[0:8], both[24:32], bias2)
    sums[32:48] = both[32:48]

    half = sums.shape[0] // 2
    own_rows = pl.ds(pl.multiple_of(core * half, 8), half)
    other_rows = pl.ds(pl.multiple_of((1 - core) * half, 8), half)
    twin = (gx + 1 - 2 * core, gy, gz)
    mine = gy * nz + gz
    chip = lax.div(gx, 2)
    pair = pltpu.make_async_remote_copy(
        src_ref=sums.at[other_rows], dst_ref=rx0, send_sem=ar_send.at[0], recv_sem=ar_recv.at[0],
        device_id=twin, device_id_type=MESH)
    pair.start()
    pair.wait_recv()
    rx1[mine] = sums[own_rows] + rx0[...]
    stage1 = [pltpu.make_async_remote_copy(
        src_ref=rx1.at[mine], dst_ref=rx1.at[mine], send_sem=ar_send.at[1], recv_sem=ar_recv.at[1],
        device_id=device(o), device_id_type=MESH) for o in plane]
    start(stage1)
    pair.wait_send()
    for x in SIDE_PLANES:
        spread(x)
    gather(0, 0)
    gather(0, BX + 1)
    start(out_copies(0, ACROSS))
    for x in MID_PLANES:
        spread(x)
    for x in range(BX):
        gather(0, x + 1)
    start(out_copies(0, WITHIN))
    wait_rows(half * len(plane), ar_recv.at[1])
    wait_rows(half * len(plane), ar_send.at[1])
    total = rx1[0]
    for i in range(1, ny * nz):
        total = total + rx1[i]
    rx2[chip] = total
    stage2 = [pltpu.make_async_remote_copy(
        src_ref=rx2.at[chip], dst_ref=rx2.at[chip], send_sem=ar_send.at[2], recv_sem=ar_recv.at[2],
        device_id=device(o), device_id_type=MESH) for o in line]
    start(stage2)
    wait_rows(HALO, send_sem.at[3])
    wait_rows(HALO, recv_sem.at[2])
    add_halo(0)
    for x in range(BX):
        for z in range(BZ):
            grad_ref[pl.ds(x * BZ + z, CH, stride=BX * BZ), :] = carried[x, z]
    stores = [pltpu.make_async_copy(a, b, store_sem.at[i]) for i, (a, b) in enumerate((
        (grad_ref, grad_out), (whole, sums_out)))]
    stores[0].start()
    wait_rows(HALO, send_sem.at[2])
    wait_rows(half * len(line), ar_recv.at[2])
    wait_rows(half * len(line), ar_send.at[2])
    total = rx2[0]
    for i in range(1, nx // 2):
        total = total + rx2[i]
    whole[own_rows] = total
    share = pltpu.make_async_remote_copy(
        src_ref=whole.at[own_rows], dst_ref=whole.at[own_rows], send_sem=ar_send.at[3], recv_sem=ar_recv.at[3],
        device_id=twin, device_id_type=MESH)
    share.start()
    share.wait()
    for c in stores[1:]:
        c.start()
    for c in stores:
        c.wait()


def write_out(scale, grad, sums, grad_out, gw1_out, gb1_out, gw2_out, gb2_out, gw1, gb1, gw2, gb2, sems):
    copies = [pltpu.make_async_copy(a, b, sems.at[i]) for i, (a, b) in enumerate((
        (grad, grad_out), (gw1, gw1_out), (gb1, gb1_out), (gw2, gw2_out), (gb2, gb2_out)))]
    copies[0].start()
    final = sums[...] * scale
    gw1[...] = final[:, 0:64]
    gb1[...] = final[16:17, 64:128]
    gw2[...] = final[0:16, 64:128]
    gb2[...] = final[24:25, 64:80]
    for c in copies[1:]:
        c.start()
    for c in copies:
        c.wait()


def body(start_state, cotangent, update_masks, first_weight, first_bias, second_weight, second_bias):
    sizes = (lax.axis_size("gx"), lax.axis_size("gy"), lax.axis_size("gz"))
    hbm = pl.BlockSpec(memory_space=pltpu.HBM)
    shapes = ((CH * BX * BZ, BY), (PERC, HID), (1, HID), (CH, HID), (1, CH))
    shapes = tuple(jax.ShapeDtypeStruct(s, F32) for s in shapes)
    scratch = [
        pltpu.VMEM((CH * BX * BZ, BY), F32),
        pltpu.VMEM((CH * BX * BZ, BY), F32),
        pltpu.VMEM((CH * BX * BZ, BY), F32),
        pltpu.VMEM((2 * BX * BZ, BY), jnp.int32),
        pltpu.VMEM((PERC, HID), F32),
        pltpu.VMEM((1, HID), F32),
        pltpu.VMEM((CH, HID), F32),
        pltpu.VMEM((1, CH), F32),
        pltpu.VMEM((2, BX + 2, BZ + 2, CH, BY), F32),
        pltpu.VMEM((2, 2, 8, 128), F32),
        pltpu.VMEM((2, 2, 3, 3, 8, 128), F32),
        pltpu.VMEM((2, BX + 2, BZ + 2, CH, BY), F32),
        pltpu.VMEM((2, 2, 2, 2, 8, 128), F32),
        pltpu.VMEM((2, 2, BZ, CH, BY), F32),
        pltpu.VMEM((2, BX, 2, CH, BY), F32),
        pltpu.VMEM((2, 2, 2, CH, BY), F32),
        pltpu.VMEM((2, 2, 3, 3, 8, 128), F32),
        pltpu.VMEM((2, BX, P_ROWS, ROW), BF16),
        pltpu.VMEM((2, BX, H_ROWS, ROW), BF16),
        pltpu.VMEM((2, BX, HID, ROW), F32),
        pltpu.VMEM((BX, 3 * HID + 3 * CH, ROW), BF16),
        pltpu.VMEM((BX, BZ, CH, BY), F32),
        pltpu.VMEM((BX + 4, 3, BZ + 2, CH, BY), F32),
        pltpu.VMEM((12, 128, 128), F32),
        pltpu.VMEM((12, 128, 128), BF16),
        pltpu.VMEM((256, 128), F32),
        pltpu.VMEM((HID, P_ROWS), BF16),
        pltpu.VMEM((CH, H_ROWS), BF16),
        pltpu.VMEM((HID, 3 * CH), BF16),
        pltpu.VMEM((PERC, 3 * HID), BF16),
        pltpu.VMEM((128, 128), F32),
        pltpu.VMEM((48, 128), F32),
        pltpu.VMEM((24, 128), F32),
        pltpu.VMEM((sizes[1] * sizes[2], 24, 128), F32),
        pltpu.VMEM((sizes[0] // 2, 24, 128), F32),
        pltpu.VMEM((48, 128), F32),
        pltpu.VMEM((BX + 2, 2, BZ, CH, BY), F32),
        pltpu.VMEM((HALO, 128), F32),
        pltpu.SemaphoreType.DMA((7,)),
        pltpu.SemaphoreType.DMA((2,)),
        pltpu.SemaphoreType.DMA((4,)),
        pltpu.SemaphoreType.DMA((4,)),
        pltpu.SemaphoreType.DMA((4,)),
        pltpu.SemaphoreType.DMA((4,)),
    ]
    outs = pl.pallas_call(
        functools.partial(kernel, sizes),
        out_shape=(shapes[0], jax.ShapeDtypeStruct((PERC, 128), F32)),
        in_specs=[hbm] * 7,
        out_specs=(hbm,) * 2,
        scratch_shapes=scratch,
        compiler_params=pltpu.CompilerParams(
            collective_id=0, has_side_effects=True, vmem_limit_bytes=60 * 1024 * 1024),
        cost_estimate=pl.CostEstimate(flops=2 * 10**8, bytes_accessed=10**6, transcendentals=524288),
        name="automaton",
    )(
        start_state.reshape(CH * BX * BZ, BY),
        cotangent.reshape(CH * BX * BZ, BY),
        update_masks.reshape(2 * BX * BZ, BY),
        first_weight, first_bias.reshape(1, HID), second_weight.T, second_bias.reshape(1, CH),
    )
    grad, gw1, gb1, gw2, gb2 = pl.pallas_call(
        functools.partial(write_out, 1.0 / math.sqrt(sizes[0] * BX * sizes[1] * BY * sizes[2] * BZ)),
        out_shape=shapes,
        in_specs=[pl.BlockSpec(memory_space=pltpu.VMEM)] * 2,
        out_specs=(hbm,) * 5,
        scratch_shapes=[pltpu.VMEM(s.shape, F32) for s in shapes[1:]] + [pltpu.SemaphoreType.DMA((5,))],
        cost_estimate=pl.CostEstimate(flops=0, bytes_accessed=600000, transcendentals=0),
        name="write_out",
    )(*outs)
    return grad.reshape(CH, BX, BZ, BY), gw1, gb1.reshape(HID), gw2.T, gb2.reshape(CH)


def solution(mesh):
    grid = P(None, "gx", "gz", "gy")
    return jax.shard_map(
        body, mesh=mesh,
        in_specs=(grid, grid, grid, P(), P(), P(), P()),
        out_specs=(grid, P(), P(), P(), P()),
        check_vma=False)
```

```python
import functools
import math

import jax
import jax.numpy as jnp
from jax import lax
from jax.experimental import pallas as pl
from jax.experimental.pallas import tpu as pltpu
from jax.sharding import PartitionSpec as P

MESH = pl.DeviceIdType.MESH
F32 = jnp.float32
BF16 = jnp.bfloat16

CH, HID, PERC = 16, 64, 48
BX, BZ, BY = 4, 8, 128
ROW = BZ * BY

P_ROWS = 2 * PERC + 16 + PERC
H_ROWS = 2 * HID + 16 + HID

DIRS = [(dx, dy, dz) for dx in (-1, 0, 1) for dy in (-1, 0, 1) for dz in (-1, 0, 1) if (dx, dy, dz) != (0, 0, 0)]
DIRS = sorted(DIRS, key=lambda d: -sum(map(abs, d)))
ACROSS = [d for d in DIRS if d[0] != 0]
WITHIN = [d for d in DIRS if d[0] == 0]
SIDE_PLANES, MID_PLANES = (0, BX - 1), tuple(range(1, BX - 1))

HALO = 2 * BZ * CH + 2 * BX * CH + 4 * CH + 18 * 8


def high(value):
    return value.astype(BF16).astype(F32)


def split3(value):
    first = high(value)
    second = high(value - first)
    return first, second, value - first - second


def span(step, length, kind):
    if step == 0:
        return pl.ds(1, length)
    if kind == "own":
        return pl.ds(1 if step < 0 else length, 1)
    return pl.ds(0 if step < 0 else length + 1, 1)


def dot(a, b):
    return lax.dot_general(a, b, (((1,), (0,)), ((), ())), preferred_element_type=F32)


def dot_nt(a, b):
    return lax.dot_general(a, b, (((1,), (1,)), ((), ())), preferred_element_type=F32)


def kernel(
    sizes,
    state_in, cot_in, mask_in, w1_in, b1_in, w2_in, b2_in,
    grad_out, sums_out,
    grad_ref,
    state_ref, cot_ref, mask_ref, w1_ref, b1_ref, w2_ref, b2_ref,
    field, packs, halos, outs, opacks, rx, rz, rc, rpacks,
    percs, hids, hidden, grads, carried, zf, placed, onehot,
    tall, l1, l2, l3, l4, turn, sums, rx0, rx1, rx2, whole, zline,
    tally, load_sem, store_sem, send_sem, recv_sem, ar_send, ar_recv,
):
    nx, ny, nz = sizes
    loads = [pltpu.make_async_copy(a, b, load_sem.at[i]) for i, (a, b) in enumerate((
        (state_in, state_ref), (w1_in, w1_ref), (b1_in, b1_ref), (w2_in, w2_ref), (b2_in, b2_ref), (cot_in, cot_ref), (mask_in, mask_ref)))]
    for c in loads:
        c.start()
    gx, gy, gz = lax.axis_index("gx"), lax.axis_index("gy"), lax.axis_index("gz")

    def device(offset):
        ox, oy, oz = offset
        return (
            lax.rem(gx + (ox % nx), nx) if ox % nx else gx,
            lax.rem(gy + (oy % ny), ny) if oy % ny else gy,
            lax.rem(gz + (oz % nz), nz) if oz % nz else gz,
        )

    def far(o):
        return -sum(min(a, n - a) for a, n in zip(o, sizes))

    plane = sorted(((0, a, b) for a in range(ny) for b in range(nz) if (a, b) != (0, 0)), key=far)
    line = sorted(((a, 0, 0) for a in range(2, nx, 2)), key=far)
    core = lax.rem(gx, 2)
    partners = []
    for o in DIRS + plane + line:
        o = (o[0] % nx, o[1] % ny, o[2] % nz)
        if o not in partners:
            partners.append(o)
    partners.sort(key=far)

    barrier = pltpu.get_barrier_semaphore()
    for o in partners:
        pl.semaphore_signal(barrier, inc=1, device_id=device(o), device_id_type=MESH)

    lane = lax.broadcasted_iota(jnp.int32, (8, 128), 1)
    sub = lax.broadcasted_iota(jnp.int32, (8, 128), 0)
    lane3 = lax.broadcasted_iota(jnp.int32, (1, 1, 128), 2)
    not_first = (lane3 > 0).astype(F32)
    not_last = (lane3 < 127).astype(F32)

    def start(copies):
        for c in copies:
            c.start()

    def wait_rows(rows, sem):
        pltpu.make_async_copy(tally.at[pl.ds(0, rows)], tally.at[pl.ds(0, rows)], sem).wait()

    def pack_state(k, x):
        turned = field[k, x + 1, pl.ds(1, BZ)].reshape(128, 128).T
        for r, row in ((x, 0), (x + 4, 127)):
            packs[k, 1, r : r + 1] = turned[row : row + 1]
            if x in SIDE_PLANES:
                packs[k, 0, r : r + 1] = turned[row : row + 1]

    loads[0].wait()
    for x in range(BX):
        for z in range(BZ):
            field[0, x + 1, z + 1] = state_ref[pl.ds(x * BZ + z, CH, stride=BX * BZ), :]
    for k in range(2):
        packs[k, 0] = jnp.zeros((8, 128), F32)
        opacks[k] = jnp.zeros_like(opacks[k])
    for x in range(BX):
        pack_state(0, x)

    def state_copies(k, dirs):
        copies = []
        for d in dirs:
            if d[1]:
                src = packs.at[k, 0 if d[0] else 1]
                dst = halos.at[k, 0 if d[1] > 0 else 1, 1 - d[0], 1 - d[2]]
            else:
                src = field.at[k, span(d[0], BX, "own"), span(d[2], BZ, "own")]
                dst = field.at[k, span(-d[0], BX, "halo"), span(-d[2], BZ, "halo")]
            copies.append(pltpu.make_async_remote_copy(
                src_ref=src, dst_ref=dst, send_sem=send_sem.at[k], recv_sem=recv_sem.at[k],
                device_id=device(d), device_id_type=MESH))
        return copies

    def out_copies(k, dirs):
        copies = []
        for d in dirs:
            at_x, at_z = pl.ds(0 if d[0] > 0 else 1, 1), pl.ds(0 if d[2] > 0 else 1, 1)
            if d[1]:
                src = opacks.at[k, 0 if d[0] else 1, 0 if d[1] < 0 else 1, 1 if d[2] else 0]
                dst = rpacks.at[k, 0 if d[1] > 0 else 1, 1 - d[0], 1 - d[2]]
            else:
                src = outs.at[k, span(d[0], BX, "halo"), span(d[2], BZ, "halo")]
                if d[0] and d[2]:
                    dst = rc.at[k, at_x, at_z]
                elif d[0]:
                    dst = rx.at[k, at_x]
                else:
                    dst = rz.at[k, :, at_z]
            copies.append(pltpu.make_async_remote_copy(
                src_ref=src, dst_ref=dst, send_sem=send_sem.at[2 + k], recv_sem=recv_sem.at[2 + k],
                device_id=device(d), device_id_type=MESH))
        return copies

    pl.semaphore_wait(barrier, len(partners))
    start(state_copies(0, DIRS))

    for c in loads[1:5]:
        c.wait()
    tall[...] = jnp.zeros_like(tall)
    w1 = w1_ref[...] * 0.125
    w1h = high(w1)
    tall[0:48, 0:64] = w1h
    tall[48:96, 0:64] = w1h
    b1 = split3(b1_ref[...])
    for s in range(3):
        tall[96 + s : 97 + s, 0:64] = b1[s]
    tall[112:160, 0:64] = w1 - w1h
    l1[...] = tall[...].T[0:64, 0:P_ROWS].astype(BF16)

    tall[...] = jnp.zeros_like(tall)
    w2t = w2_ref[...]
    tall[0:16, 0:64] = w2t
    w2 = tall[...].T[0:64, 0:16]
    tall[...] = jnp.zeros_like(tall)
    w2h = high(w2)
    tall[0:64, 0:16] = w2h
    tall[64:128, 0:16] = w2h
    b2 = split3(b2_ref[...])
    for s in range(3):
        tall[128 + s : 129 + s, 0:16] = b2[s]
    tall[144:208, 0:16] = w2 - w2h
    l2[...] = tall[...].T[0:16, 0:H_ROWS].astype(BF16)

    tall[...] = jnp.zeros_like(tall)
    tall[0:48, 0:64] = -w1
    w1t = tall[...].T[0:64, 0:48]
    tall[...] = jnp.zeros_like(tall)
    w1th = high(w1t)
    tall[0:64, 0:48] = w1t - w1th
    tall[64:128, 0:48] = w1th
    tall[128:192, 0:48] = w1th
    l4[...] = tall[...].T[0:48, 0:192].astype(BF16)

    tall[...] = jnp.zeros_like(tall)
    w2th = high(w2t)
    tall[0:16, 0:64] = w2th
    tall[16:32, 0:64] = w2th
    tall[32:48, 0:64] = w2t - w2th
    l3[...] = tall[...].T[0:64, 0:48].astype(BF16)

    kk = lax.broadcasted_iota(jnp.int32, (128, 128), 0)
    yy = lax.broadcasted_iota(jnp.int32, (128, 128), 1)
    feature = lax.rem(lax.div(kk, 8), 3)
    row8 = lax.rem(kk, 8)
    hit = jnp.logical_and(kk < 72, yy == jnp.where(row8 < 4, 127, 0))
    for x in range(BX):
        for f in range(3):
            sign = jnp.where(row8 < 4, 1.0, -1.0) if f == 1 else 1.0
            onehot[x * 3 + f] = jnp.where(
                jnp.logical_and(hit, jnp.logical_and(feature == f, lax.rem(row8, 4) == x)), sign, 0.0
            ).astype(BF16)
    turn[...] = jnp.zeros_like(turn)
    for k in range(2):
        for x in range(BX):
            percs[k, x, 2 * PERC : 2 * PERC + 16, :] = jnp.ones((16, ROW), BF16)
            hids[k, x, 2 * HID : 2 * HID + 16, :] = jnp.ones((16, ROW), BF16)
    for x in (0, 1, BX + 2, BX + 3):
        zf[x] = jnp.zeros_like(zf[x])
    for c in loads[5:]:
        c.wait()
    for x in range(BX):
        for z in range(BZ):
            carried[x, z] = cot_ref[pl.ds(x * BZ + z, CH, stride=BX * BZ), :]

    low_x, top_x = (gx > 0).astype(F32), (gx < nx - 1).astype(F32)
    low_y, top_y = (gy > 0).astype(F32), (gy < ny - 1).astype(F32)
    low_z, top_z = (gz > 0).astype(F32), (gz < nz - 1).astype(F32)
    in_x, in_z = (low_x, 1.0, top_x), (low_z, 1.0, top_z)

    def halves(value):
        hi = value.astype(BF16)
        return hi, (value - hi.astype(F32)).astype(BF16)

    def place(rows24, features):
        parts = split3(rows24)
        n = 8 * features
        for s in range(3):
            turn[24 * s : 24 * s + n, :] = parts[s]
        turned = turn[...].T.astype(BF16)
        for x in range(BX):
            for f in range(features):
                placed[x * 3 + f] = dot(turned, onehot[x * 3 + f])

    def clear_outside(k):
        @pl.when(gx == 0)
        def _():
            field[k, 0] = jnp.zeros_like(field[k, 0])
        @pl.when(gx == nx - 1)
        def _():
            field[k, BX + 1] = jnp.zeros_like(field[k, BX + 1])
        @pl.when(gz == 0)
        def _():
            field[k, :, 0] = jnp.zeros_like(field[k, :, 0])
        @pl.when(gz == nz - 1)
        def _():
            field[k, :, BZ + 1] = jnp.zeros_like(field[k, :, BZ + 1])

    def filter_columns(k):
        grid = {}
        for ix in range(3):
            for iz in range(3):
                tile = jnp.where(sub < 4, halos[k, 1, ix, iz] * top_y, halos[k, 0, ix, iz] * low_y)
                grid[ix, iz] = tile * (in_x[ix] * in_z[iz])
        xs, xd = [], []
        for iz in range(3):
            mid = grid[1, iz]
            after = pltpu.roll(jnp.where(lax.rem(sub, 4) == 0, pltpu.roll(grid[2, iz], 4, 0), mid), 7, 0)
            before = pltpu.roll(jnp.where(lax.rem(sub, 4) == 3, pltpu.roll(grid[0, iz], 4, 0), mid), 1, 0)
            xs.append(before + 2.0 * mid + after)
            xd.append(after - before)

        def around(t):
            above = pltpu.roll(jnp.where(lane < 16, t[2], t[1]), 112, 1)
            below = pltpu.roll(jnp.where(lane >= 112, t[0], t[1]), 16, 1)
            return below, above

        d_below, d_above = around(xd)
        s_below, s_above = around(xs)
        place(jnp.concatenate([
            d_below + 2.0 * xd[1] + d_above,
            s_below + 2.0 * xs[1] + s_above,
            s_above - s_below], axis=0), 3)

    ready = set()

    def forward(k, x):
        zs, zd = [], []
        for i in range(x, x + 3):
            if (k, i) not in ready:
                ready.add((k, i))
                v = field[k, i]
                zs.append(v[0:8] + 2.0 * v[1:9] + v[2:10])
                zd.append(v[2:10] - v[0:8])
                zline[i, 0], zline[i, 1] = zs[-1], zd[-1]
            else:
                zs.append(zline[i, 0])
                zd.append(zline[i, 1])
        b = zs[2] - zs[0]
        a = zs[0] + 2.0 * zs[1] + zs[2]
        c = zd[0] + 2.0 * zd[1] + zd[2]
        up = lambda t: pltpu.roll(t, 127, 2) * not_last
        down = lambda t: pltpu.roll(t, 1, 2) * not_first
        features = (
            2.0 * b + up(b) + down(b),
            up(a) - down(a),
            2.0 * c + up(c) + down(c),
        )
        for f in range(3):
            perc = features[f] + placed[x * 3 + f].reshape(BZ, CH, BY)
            flat = jnp.concatenate([perc[z] for z in range(BZ)], axis=1)
            hi, lo = halves(flat)
            percs[k, x, f * 16 : f * 16 + 16] = hi
            percs[k, x, 48 + f * 16 : 64 + f * 16] = lo
            percs[k, x, 112 + f * 16 : 128 + f * 16] = hi
        hid = jnp.tanh(dot(l1[...], percs[k, x]))
        hidden[k, x] = hid
        hi, lo = halves(hid)
        hids[k, x, 0:64] = hi
        hids[k, x, 64:128] = lo
        hids[k, x, 144:208] = hi

    def advance(x):
        update = dot(l2[...], hids[0, x])
        mask = mask_ref[x * BZ : (x + 1) * BZ, :].astype(F32)
        for z in range(BZ):
            field[1, x + 1, z + 1] = field[0, x + 1, z + 1] + mask[z : z + 1] * update[:, z * BY : (z + 1) * BY]
        pack_state(1, x)

    def cells(k, x):
        mask = mask_ref[(k * BX + x) * BZ : (k * BX + x + 1) * BZ, :].astype(F32)
        g = carried[x]
        du = jnp.concatenate([mask[z : z + 1] * g[z] for z in range(BZ)], axis=1)
        hi, lo = halves(du)
        grads[x, 192:208] = hi
        grads[x, 208:224] = lo
        grads[x, 224:240] = hi
        hid = hidden[k, x]
        dz = dot(l3[...], grads[x, 192:240]) * (1.0 - hid * hid)
        hi, lo = halves(dz)
        grads[x, 0:64] = hi
        grads[x, 64:128] = hi
        grads[x, 128:192] = lo

    def spread(x):
        dp = dot(l4[...], grads[x, 0:192])
        zero = jnp.zeros((2, CH, BY), F32)
        for f in range(3):
            q = jnp.concatenate(
                [zero] + [dp[f * 16 : f * 16 + 16, z * BY : (z + 1) * BY].reshape(1, CH, BY) for z in range(BZ)] + [zero], axis=0)
            zf[x + 2, f] = q[2:12] - q[0:10] if f == 2 else q[0:10] + 2.0 * q[1:11] + q[2:12]

    def gather(k, xo):
        pr = zf[xo + 2, 0] - zf[xo, 0] + zf[xo, 2] + 2.0 * zf[xo + 1, 2] + zf[xo + 2, 2]
        q = zf[xo, 1] + 2.0 * zf[xo + 1, 1] + zf[xo + 2, 1]
        up, down = pr + q, pr - q
        outs[k, xo] = 2.0 * pr + pltpu.roll(down, 1, 2) * not_first + pltpu.roll(up, 127, 2) * not_last
        both = jnp.where(lane3 == 0, up, down)
        main = both[1:9].reshape(128, 128).T
        side = jnp.concatenate([both[0], both[9]], axis=0)
        side = side.T
        tile = 0 if xo in (0, BX + 1) else 1
        for s, r in ((0, 0), (1, 127)):
            opacks[k, tile, s, 0, xo : xo + 1] = main[r : r + 1]
            opacks[k, tile, s, 1, xo : xo + 1, 0:32] = side[r : r + 1]

    def add_halo(k):
        total = jnp.zeros((8, 128), F32)
        for iy in range(2):
            base = 4 if iy == 0 else 0
            in_y = low_y if iy == 0 else top_y
            for ix in range(3):
                part = jnp.zeros((8, 128), F32)
                for iz in range(3):
                    if iz == 1:
                        t = rpacks[k, iy, ix, iz]
                    else:
                        t = pltpu.roll(rpacks[k, iy, ix, iz], 112, 1)
                        t = jnp.where(lane < 16 if iz == 0 else lane >= 112, t, 0.0)
                    part = part + t * (in_y * in_x[ix] * in_z[iz])
                if ix == 1:
                    part = jnp.where(lax.div(sub, 4) == base // 4, pltpu.roll(part, 3 if iy == 0 else 7, 0), 0.0)
                else:
                    row = base if ix == 0 else base + 3
                    part = jnp.where(sub == row, pltpu.roll(part, 7 if iy == 0 else 3, 0), 0.0)
                total = total + part
        place(total, 1)

        def body(x, _):
            carried[x] = carried[x] + outs[k, x + 1, pl.ds(1, BZ)] + placed[x * 3].reshape(BZ, CH, BY)
            return 0
        lax.fori_loop(0, BX, body, 0, unroll=True)
        for ix in range(2):
            x = 0 if ix == 0 else BX - 1
            m = low_x if ix == 0 else top_x
            carried[x] = carried[x] + rx[k, ix] * m
            for iz in range(2):
                z = 0 if iz == 0 else BZ - 1
                carried[x, z] = carried[x, z] + rc[k, ix, iz] * (m * (low_z if iz == 0 else top_z))
        for iz in range(2):
            z = 0 if iz == 0 else BZ - 1
            m = low_z if iz == 0 else top_z
            carried[:, z] = carried[:, z] + rz[k, :, iz] * m

    def weight_grads(k):
        def body(x, acc):
            g1, g2 = acc
            g1 = g1 + dot_nt(percs[k, x, 0:112], grads[x, 64:224])
            g2 = g2 + dot_nt(grads[x, 192:224], hids[k, x, 0:128])
            return g1, g2
        return lax.fori_loop(0, BX, body, (jnp.zeros((112, 160), F32), jnp.zeros((32, 128), F32)), unroll=True)

    wait_rows(HALO, recv_sem.at[0])
    clear_outside(0)
    filter_columns(0)
    for x in SIDE_PLANES:
        forward(0, x)
        advance(x)
    start(state_copies(1, ACROSS))
    for x in MID_PLANES:
        forward(0, x)
        advance(x)
    start(state_copies(1, WITHIN))
    wait_rows(HALO, send_sem.at[0])
    wait_rows(HALO, recv_sem.at[1])
    clear_outside(1)
    filter_columns(1)
    for x in SIDE_PLANES:
        forward(1, x)
        cells(1, x)
    for x in SIDE_PLANES:
        spread(x)
    gather(1, 0)
    gather(1, BX + 1)
    start(out_copies(1, ACROSS))
    for x in MID_PLANES:
        forward(1, x)
        cells(1, x)
        spread(x)
    for x in range(BX):
        gather(1, x + 1)
    start(out_copies(1, WITHIN))
    ga1, ga2 = weight_grads(1)
    wait_rows(HALO, send_sem.at[1])
    wait_rows(HALO, recv_sem.at[3])
    add_halo(1)
    for x in range(BX):
        cells(0, x)
    gb1, gb2 = weight_grads(0)
    g1, g2 = ga1 + gb1, ga2 + gb2

    both = (g1[0:48] + g1[48:96])[:, 0:128]
    both = (both + pltpu.roll(both, 64, 1)) * 0.125
    bias1 = g1[96:104, 0:128]
    bias1 = bias1 + pltpu.roll(bias1, 64, 1)
    bias2 = jnp.concatenate([g1[96:104, 128:160], jnp.zeros((8, 96), F32)], axis=1)
    bias2 = pltpu.roll(bias2, 64, 1) + pltpu.roll(bias2, 48, 1)
    second_w = g2[0:16] + g2[16:32]
    second_w = second_w + pltpu.roll(second_w, 64, 1)
    left = lax.broadcasted_iota(jnp.int32, (16, 128), 1) < 64
    sums[0:16] = jnp.where(left, both[0:16], second_w)
    sums[16:24] = jnp.where(left[0:8], both[16:24], bias1)
    sums[24:32] = jnp.where(left[0:8], both[24:32], bias2)
    sums[32:48] = both[32:48]

    half = sums.shape[0] // 2
    own_rows = pl.ds(pl.multiple_of(core * half, 8), half)
    other_rows = pl.ds(pl.multiple_of((1 - core) * half, 8), half)
    twin = (gx + 1 - 2 * core, gy, gz)
    mine = gy * nz + gz
    chip = lax.div(gx, 2)
    pair = pltpu.make_async_remote_copy(
        src_ref=sums.at[other_rows], dst_ref=rx0, send_sem=ar_send.at[0], recv_sem=ar_recv.at[0],
        device_id=twin, device_id_type=MESH)
    pair.start()
    pair.wait_recv()
    rx1[mine] = sums[own_rows] + rx0[...]
    stage1 = [pltpu.make_async_remote_copy(
        src_ref=rx1.at[mine], dst_ref=rx1.at[mine], send_sem=ar_send.at[1], recv_sem=ar_recv.at[1],
        device_id=device(o), device_id_type=MESH) for o in plane]
    start(stage1)
    pair.wait_send()
    for x in SIDE_PLANES:
        spread(x)
    gather(0, 0)
    gather(0, BX + 1)
    start(out_copies(0, ACROSS))
    for x in MID_PLANES:
        spread(x)
    for x in range(BX):
        gather(0, x + 1)
    start(out_copies(0, WITHIN))
    wait_rows(half * len(plane), ar_recv.at[1])
    wait_rows(half * len(plane), ar_send.at[1])
    total = rx1[0]
    for i in range(1, ny * nz):
        total = total + rx1[i]
    rx2[chip] = total
    stage2 = [pltpu.make_async_remote_copy(
        src_ref=rx2.at[chip], dst_ref=rx2.at[chip], send_sem=ar_send.at[2], recv_sem=ar_recv.at[2],
        device_id=device(o), device_id_type=MESH) for o in line]
    start(stage2)
    wait_rows(HALO, send_sem.at[3])
    wait_rows(HALO, recv_sem.at[2])
    add_halo(0)
    for x in range(BX):
        for z in range(BZ):
            grad_ref[pl.ds(x * BZ + z, CH, stride=BX * BZ), :] = carried[x, z]
    stores = [pltpu.make_async_copy(a, b, store_sem.at[i]) for i, (a, b) in enumerate((
        (grad_ref, grad_out), (whole, sums_out)))]
    stores[0].start()
    wait_rows(HALO, send_sem.at[2])
    wait_rows(half * len(line), ar_recv.at[2])
    wait_rows(half * len(line), ar_send.at[2])
    total = rx2[0]
    for i in range(1, nx // 2):
        total = total + rx2[i]
    whole[own_rows] = total
    share = pltpu.make_async_remote_copy(
        src_ref=whole.at[own_rows], dst_ref=whole.at[own_rows], send_sem=ar_send.at[3], recv_sem=ar_recv.at[3],
        device_id=twin, device_id_type=MESH)
    share.start()
    share.wait()
    for c in stores[1:]:
        c.start()
    for c in stores:
        c.wait()


def write_out(scale, grad, sums, grad_out, gw1_out, gb1_out, gw2_out, gb2_out, gw1, gb1, gw2, gb2, sems):
    copies = [pltpu.make_async_copy(a, b, sems.at[i]) for i, (a, b) in enumerate((
        (grad, grad_out), (gw1, gw1_out), (gb1, gb1_out), (gw2, gw2_out), (gb2, gb2_out)))]
    copies[0].start()
    final = sums[...] * scale
    gw1[...] = final[:, 0:64]
    gb1[...] = final[16:17, 64:128]
    gw2[...] = final[0:16, 64:128]
    gb2[...] = final[24:25, 64:80]
    for c in copies[1:]:
        c.start()
    for c in copies:
        c.wait()


def body(start_state, cotangent, update_masks, first_weight, first_bias, second_weight, second_bias):
    sizes = (lax.axis_size("gx"), lax.axis_size("gy"), lax.axis_size("gz"))
    hbm = pl.BlockSpec(memory_space=pltpu.HBM)
    shapes = ((CH * BX * BZ, BY), (PERC, HID), (1, HID), (CH, HID), (1, CH))
    shapes = tuple(jax.ShapeDtypeStruct(s, F32) for s in shapes)
    scratch = [
        pltpu.VMEM((CH * BX * BZ, BY), F32),
        pltpu.VMEM((CH * BX * BZ, BY), F32),
        pltpu.VMEM((CH * BX * BZ, BY), F32),
        pltpu.VMEM((2 * BX * BZ, BY), jnp.int32),
        pltpu.VMEM((PERC, HID), F32),
        pltpu.VMEM((1, HID), F32),
        pltpu.VMEM((CH, HID), F32),
        pltpu.VMEM((1, CH), F32),
        pltpu.VMEM((2, BX + 2, BZ + 2, CH, BY), F32),
        pltpu.VMEM((2, 2, 8, 128), F32),
        pltpu.VMEM((2, 2, 3, 3, 8, 128), F32),
        pltpu.VMEM((2, BX + 2, BZ + 2, CH, BY), F32),
        pltpu.VMEM((2, 2, 2, 2, 8, 128), F32),
        pltpu.VMEM((2, 2, BZ, CH, BY), F32),
        pltpu.VMEM((2, BX, 2, CH, BY), F32),
        pltpu.VMEM((2, 2, 2, CH, BY), F32),
        pltpu.VMEM((2, 2, 3, 3, 8, 128), F32),
        pltpu.VMEM((2, BX, P_ROWS, ROW), BF16),
        pltpu.VMEM((2, BX, H_ROWS, ROW), BF16),
        pltpu.VMEM((2, BX, HID, ROW), F32),
        pltpu.VMEM((BX, 3 * HID + 3 * CH, ROW), BF16),
        pltpu.VMEM((BX, BZ, CH, BY), F32),
        pltpu.VMEM((BX + 4, 3, BZ + 2, CH, BY), F32),
        pltpu.VMEM((12, 128, 128), F32),
        pltpu.VMEM((12, 128, 128), BF16),
        pltpu.VMEM((256, 128), F32),
        pltpu.VMEM((HID, P_ROWS), BF16),
        pltpu.VMEM((CH, H_ROWS), BF16),
        pltpu.VMEM((HID, 3 * CH), BF16),
        pltpu.VMEM((PERC, 3 * HID), BF16),
        pltpu.VMEM((128, 128), F32),
        pltpu.VMEM((48, 128), F32),
        pltpu.VMEM((24, 128), F32),
        pltpu.VMEM((sizes[1] * sizes[2], 24, 128), F32),
        pltpu.VMEM((sizes[0] // 2, 24, 128), F32),
        pltpu.VMEM((48, 128), F32),
        pltpu.VMEM((BX + 2, 2, BZ, CH, BY), F32),
        pltpu.VMEM((HALO, 128), F32),
        pltpu.SemaphoreType.DMA((7,)),
        pltpu.SemaphoreType.DMA((2,)),
        pltpu.SemaphoreType.DMA((4,)),
        pltpu.SemaphoreType.DMA((4,)),
        pltpu.SemaphoreType.DMA((4,)),
        pltpu.SemaphoreType.DMA((4,)),
    ]
    outs = pl.pallas_call(
        functools.partial(kernel, sizes),
        out_shape=(shapes[0], jax.ShapeDtypeStruct((PERC, 128), F32)),
        in_specs=[hbm] * 7,
        out_specs=(hbm,) * 2,
        scratch_shapes=scratch,
        compiler_params=pltpu.CompilerParams(
            collective_id=0, has_side_effects=True, vmem_limit_bytes=60 * 1024 * 1024),
        cost_estimate=pl.CostEstimate(flops=2 * 10**8, bytes_accessed=10**6, transcendentals=524288),
        name="automaton",
    )(
        start_state.reshape(CH * BX * BZ, BY),
        cotangent.reshape(CH * BX * BZ, BY),
        update_masks.reshape(2 * BX * BZ, BY),
        first_weight, first_bias.reshape(1, HID), second_weight.T, second_bias.reshape(1, CH),
    )
    grad, gw1, gb1, gw2, gb2 = pl.pallas_call(
        functools.partial(write_out, 1.0 / math.sqrt(sizes[0] * BX * sizes[1] * BY * sizes[2] * BZ)),
        out_shape=shapes,
        in_specs=[pl.BlockSpec(memory_space=pltpu.VMEM)] * 2,
        out_specs=(hbm,) * 5,
        scratch_shapes=[pltpu.VMEM(s.shape, F32) for s in shapes[1:]] + [pltpu.SemaphoreType.DMA((5,))],
        cost_estimate=pl.CostEstimate(flops=0, bytes_accessed=600000, transcendentals=0),
        name="write_out",
    )(*outs)
    return grad.reshape(CH, BX, BZ, BY), gw1, gb1.reshape(HID), gw2.T, gb2.reshape(CH)


def solution(mesh):
    grid = P(None, "gx", "gz", "gy")
    return jax.shard_map(
        body, mesh=mesh,
        in_specs=(grid, grid, grid, P(), P(), P(), P()),
        out_specs=(grid, P(), P(), P(), P()),
        check_vma=False)
```
